32 devices in a mesh: dp: 4 (over z), seq: 8 (over y, x, core).
Axes of the slice: x: 2, y: 2, z: 4, core: 2. Of those that a mesh axis runs over, the one named last changes fastest.
Arguments:
- tokens: bfloat16 [8, 4096, 512], P('dp', 'seq'), may hold values from -6 to 6
- prefix: int32 [8], P('dp'), may hold values from 409 to 2048
- neighbours: int32 [8, 4096, 4], P('dp', 'seq'), may hold values from 0 to 1023
- table: bfloat16 [1024, 512], P('seq'), may hold values from -6 to 6
- attn_gain: bfloat16 [512], P(('dp', 'seq')), may hold values from 0.5 to 1.5
- w_query: bfloat16 [512, 512], P(('dp', 'seq')), may hold values from -0.25 to 0.25
- w_key: bfloat16 [512, 512], P(('dp', 'seq')), may hold values from -0.25 to 0.25
- w_value: bfloat16 [512, 512], P(('dp', 'seq')), may hold values from -0.25 to 0.25
- gate_vector: bfloat16 [512], P(('dp', 'seq')), may hold values from -6 to 6
- w_output: bfloat16 [512, 512], P(('dp', 'seq')), may hold values from -0.5 to 0.5
- ffn_gain: bfloat16 [512], P(('dp', 'seq')), may hold values from 0.5 to 1.5
- w_inner: bfloat16 [512, 2048], P(('dp', 'seq')), may hold values from -0.25 to 0.25
- w_outer: bfloat16 [2048, 512], P(('dp', 'seq')), may hold values from -0.125 to 0.125
- cotangent: bfloat16 [8, 4096, 512], P('dp', 'seq'), may hold values from -6 to 6
Outputs:
- output: bfloat16 [8, 4096, 512], P('dp', 'seq')
- input_grad: float32 [8, 4096, 512], P('dp', 'seq')
- grad_attn_gain: float32 [512], P(('dp', 'seq'))
- grad_w_query: float32 [512, 512], P(('dp', 'seq'))
- grad_w_key: float32 [512, 512], P(('dp', 'seq'))
- grad_w_value: float32 [512, 512], P(('dp', 'seq'))
- grad_gate_vector: float32 [512], P(('dp', 'seq'))
- grad_w_output: float32 [512, 512], P(('dp', 'seq'))
- grad_ffn_gain: float32 [512], P(('dp', 'seq'))
- grad_w_inner: float32 [512, 2048], P(('dp', 'seq'))
- grad_w_outer: float32 [2048, 512], P(('dp', 'seq'))
The draws below stay inside these ranges and needn't reach their ends.
All inputs are finite; a program needn't handle non-finite values.
Results may differ from the reference program's by a relative error of at most 0.012.
Values may be sent and summed in bfloat16 or wider, within the bound.
A program may use at most 192 MiB of HBM per device.

```python
from functools import partial
import jax
import jax.numpy as jnp
from jax import lax

D = 512
HEADS = 8
HD = 64
FF = 2048
KNN = 4
SEG = 512
LENGTH = 4096
SEQS = 8
TABLE = 1024


def plant(entries, own_key, least, top_value):
    shape = entries.shape
    index_at = [jax.random.randint(jax.random.fold_in(own_key, axis), (), 0, shape[axis]) for axis in range(len(shape))]
    entries = entries.at[tuple(index_at)].set(least)
    longest = shape.index(max(shape))
    index_at[longest] = (index_at[longest] + 1) % shape[longest]
    return entries.at[tuple(index_at)].set(top_value)


def level_of(stream_key, shape, shards, smallest, top_value):
    level = 1.0
    for position, parts in shards:
        steps = jax.random.uniform(jax.random.fold_in(jax.random.fold_in(stream_key, 6), position), (parts,), jnp.float32, smallest / len(shards), top_value / len(shards))
        level = level * jnp.repeat(jnp.exp(steps), shape[position] // parts).reshape((-1,) + (1,) * (len(shape) - 1 - position))
    return level


def centred(key, extent, scale, limit, cuts=(), kind=jnp.bfloat16):
    factor_of = level_of(key, extent, cuts, -0.22, 0.18) if cuts else 1.0
    drawn = jax.random.normal(key, extent, jnp.float32) * scale * factor_of
    return jnp.minimum(jnp.maximum(drawn, -limit), limit).astype(kind)


def setup_inputs(seed: int = 0) -> dict:
    keys = jax.random.split(jax.random.key(seed), 15)
    tokens = centred(keys[0], (SEQS, LENGTH, D), 1.0, 6.0, ((0, 4), (1, 8)))
    prefix = plant(jax.random.randint(keys[1], (SEQS,), LENGTH // 10, LENGTH // 2 + 1), jax.random.fold_in(keys[1], 1), LENGTH // 10, (LENGTH // 2 + 1) - 1).astype(jnp.int32)
    neighbours = plant(jax.random.randint(keys[2], (SEQS, LENGTH, KNN), 0, TABLE), jax.random.fold_in(keys[2], 1), 0, TABLE - 1).astype(jnp.int32)
    table = centred(keys[3], (TABLE, D), 1.0, 6.0, ((0, 8),))
    attn_gain = jnp.clip(1.0 + 0.1 * jax.random.normal(keys[4], (D,), jnp.float32), 0.5, 1.5).astype(jnp.bfloat16)
    w_query = centred(keys[5], (D, D), D ** -0.5, 0.25, ((0, 32),))
    w_key = centred(keys[6], (D, D), D ** -0.5, 0.25, ((0, 32),))
    w_value = centred(keys[7], (D, D), D ** -0.5, 0.25, ((0, 32),))
    gate_vector = centred(keys[8], (D,), 1.0, 6.0, ((0, 32),))
    w_output = centred(keys[9], (D, D), (D // 4) ** -0.5, 0.5, ((0, 32),))
    ffn_gain = jnp.clip(1.0 + 0.1 * jax.random.normal(keys[10], (D,), jnp.float32), 0.5, 1.5).astype(jnp.bfloat16)
    w_inner = centred(keys[11], (D, FF), D ** -0.5, 0.25, ((0, 32),))
    w_outer = centred(keys[12], (FF, D), FF ** -0.5, 0.125, ((0, 32),))
    cotangent = centred(keys[13], (SEQS, LENGTH, D), 1.0, 6.0, ((0, 4), (1, 8)))
    return {"tokens": tokens, "prefix": prefix, "neighbours": neighbours, "table": table, "attn_gain": attn_gain, "w_query": w_query, "w_key": w_key, "w_value": w_value, "gate_vector": gate_vector, "w_output": w_output, "ffn_gain": ffn_gain, "w_inner": w_inner, "w_outer": w_outer, "cotangent": cotangent}


epsilon = 1e-06
highest = lax.Precision.HIGHEST
masked_floor = -1000000000.0

@jax.custom_vjp
def low(v):
    return lax.optimization_barrier(v.astype(jnp.bfloat16)).astype(jnp.float32)

@jax.custom_vjp
def low_back(v):
    return v

def low_keep(v):
    return (low(v), None)

def low_pass(kept, grad):
    return (grad,)

def back_keep(v):
    return (v, None)

def back_low(kept, grad):
    return (low(grad),)
low.defvjp(low_keep, low_pass)
low_back.defvjp(back_keep, back_low)

def matmul_high(left, right):
    return jnp.dot(left, right, precision=highest)

def rms_scale(values):
    return lax.rsqrt(lax.optimization_barrier(jnp.mean(values * values, axis=-1, keepdims=True)) + epsilon)

def softmax_last(scores):
    row_max = lax.optimization_barrier(jnp.max(scores, axis=-1, keepdims=True))
    exponent = jnp.exp(scores - row_max)
    return exponent / lax.optimization_barrier(jnp.sum(exponent, axis=-1, keepdims=True))

def masked_softmax(scores, visible):
    clamped = jnp.where(visible, scores, masked_floor)
    row_max = lax.optimization_barrier(jnp.max(clamped, axis=-1, keepdims=True))
    exponent = jnp.where(visible, jnp.exp(clamped - row_max), 0.0)
    return exponent / lax.optimization_barrier(jnp.sum(exponent, axis=-1, keepdims=True))

def with_memory(rows, seg_count):
    blocks = rows.reshape(seg_count, SEG, D)
    earlier = jnp.concatenate([jnp.zeros((1, SEG, D), jnp.float32).astype(rows.dtype), blocks[:-1]], axis=0)
    return jnp.concatenate([earlier, blocks], axis=1)

def segment_attention(prefix_len, operands):
    queries, key_rows, value_rows, segment = operands
    queries_h = queries.reshape(SEG, HEADS, HD).transpose(1, 0, 2)
    keys_h = key_rows.reshape(2 * SEG, HEADS, HD).transpose(1, 0, 2)
    values_h = value_rows.reshape(2 * SEG, HEADS, HD).transpose(1, 0, 2)
    scores = low_back(jnp.einsum('hqd,hkd->hqk', queries_h, keys_h, precision=highest) * 0.125)
    segment_i = segment.astype(jnp.int32)
    prefix_i = prefix_len.astype(jnp.int32)
    query_pos = (segment_i * SEG + lax.iota(jnp.int32, SEG)).astype(jnp.int32)
    key_pos = ((segment_i - 1) * SEG + lax.iota(jnp.int32, 2 * SEG)).astype(jnp.int32)
    visible = (key_pos[None, :] >= 0) & ((key_pos[None, :] <= query_pos[:, None]) | (query_pos[:, None] < prefix_i) & (key_pos[None, :] < prefix_i))
    attn_probs = low(masked_softmax(scores, visible[None]))
    mixed_out = jnp.einsum('hqk,hkd->hqd', attn_probs, values_h, precision=highest)
    return mixed_out.transpose(1, 0, 2).reshape(SEG, D)

def block_forward(prefix_len, near_rows, tokens_f, attn_gain, w_query, w_key, w_value, gate_vector, w_output, ffn_gain, w_inner, w_outer):
    length = tokens_f.shape[0]
    seg_count = length // SEG
    normed_in = low(tokens_f * rms_scale(tokens_f) * attn_gain)
    query_b = low(low_back(matmul_high(normed_in, w_query)))
    key_b = low(low_back(matmul_high(normed_in, w_key)))
    value_b = low(low_back(matmul_high(normed_in, w_value)))
    attend = jax.checkpoint(partial(segment_attention, prefix_len))
    segments = lax.iota(jnp.int32, seg_count)
    local = lax.map(attend, (query_b.reshape(seg_count, SEG, D), with_memory(key_b, seg_count), with_memory(value_b, seg_count), segments))
    local = low_back(local.reshape(length, HEADS, HD))
    query_t = query_b.reshape(length, HEADS, HD)
    near_h = near_rows.reshape(length, KNN, HEADS, HD)
    near_weights = softmax_last(jnp.einsum('lhd,lkhd->lhk', query_t, near_h, precision=highest) * 0.125)
    recalled = jnp.einsum('lhk,lkhd->lhd', near_weights, near_h, precision=highest)
    gate_open = jax.nn.sigmoid(lax.optimization_barrier(jnp.sum(local * gate_vector.reshape(HEADS, HD), axis=-1, keepdims=True)))
    blended_b = low((gate_open * recalled + (1.0 - gate_open) * local).reshape(length, D))
    middle = tokens_f + low_back(matmul_high(blended_b, w_output))
    ffn_in = low(middle * rms_scale(middle) * ffn_gain)
    hidden_pre = low_back(matmul_high(ffn_in, w_inner))
    hidden_b = low(jax.nn.gelu(hidden_pre, approximate=True))
    return middle + low_back(matmul_high(hidden_b, w_outer))

def reference(tokens, prefix, neighbours, table, attn_gain, w_query, w_key, w_value, gate_vector, w_output, ffn_gain, w_inner, w_outer, cotangent):
    weights = tuple((weight.astype(jnp.float32) for weight in (attn_gain, w_query, w_key, w_value, gate_vector, w_output, ffn_gain, w_inner, w_outer)))
    table_f = table.astype(jnp.float32)

    def per_sequence(carry, operands):
        tokens_row, prefix_len, rows_idx, cot_row = operands
        near_rows = jnp.take(table_f, rows_idx.astype(jnp.int32), axis=0)
        forward = partial(block_forward, prefix_len.astype(jnp.int32), near_rows)
        result, pullback = jax.vjp(forward, tokens_row.astype(jnp.float32), *weights)
        grads = pullback(cot_row.astype(jnp.float32))
        carry = tuple((running + increment.astype(jnp.float32) for running, increment in zip(carry, grads[1:])))
        return (carry, (result.astype(jnp.bfloat16), grads[0].astype(jnp.float32)))
    zeros_init = tuple((jnp.zeros(weight.shape, jnp.float32) for weight in weights))
    sums, stacked = lax.scan(per_sequence, zeros_init, (tokens, prefix.astype(jnp.int32), neighbours.astype(jnp.int32), cotangent))
    return (stacked[0], stacked[1], sums[0], sums[1], sums[2], sums[3], sums[4], sums[5], sums[6], sums[7], sums[8])
```

```python
import jax
import jax.numpy as jnp
from jax import lax
from jax.experimental import pallas as pl
from jax.experimental.pallas import tpu as pltpu
from jax.sharding import PartitionSpec as P

D = 512
HEADS = 8
HD = 64
KNN = 4
SEG = 512
FF = 2048
PAIRS = 4
NB = 2
MESH = pl.DeviceIdType.MESH

epsilon = 1e-06
far = 1e30
f32 = jnp.float32
bf16 = jnp.bfloat16


def mm(left, right, over_left, over_right):
    return lax.dot_general(
        left, right, (((over_left,), (over_right,)), ((), ())), preferred_element_type=f32
    )


class Place:
    def __init__(self, dpn):
        self.dpn = dpn
        self.dp = lax.axis_index("dp")
        self.s = lax.axis_index("seq")
        self.c = self.s % 2
        self.x = (self.s // 2) % 2
        self.y = self.s // 4

    def across(self, axis):
        if axis == "c":
            return (self.dp, self.s + 1 - 2 * self.c)
        if axis == "x":
            return (self.dp, self.s + 2 * (1 - 2 * self.x))
        return (self.dp, self.s + 4 * (1 - 2 * self.y))

    def along(self, step):
        return ((self.dp + step) % self.dpn, self.s)


def remote(src, dst, send, recv, device):
    return pltpu.make_async_remote_copy(
        src_ref=src, dst_ref=dst, send_sem=send, recv_sem=recv, device_id=device, device_id_type=MESH
    )


class Gather:
    def __init__(self, place, buf, send, recv, order, flat=False):
        self.place, self.buf, self.send, self.recv = place, buf, send, recv
        self.order = order if flat else ("z",) + order
        self.flat = flat
        self.live = []

    def copies(self, stage):
        p = self.place
        axis = self.order[stage]
        if axis == "z":
            own = self.buf.at[p.dp, p.y, p.x, p.c]
            return [
                remote(own, own, self.send.at[k], self.recv.at[k], p.along(k + 1))
                for k in range(p.dpn - 1)
            ]
        done = self.order[:stage]
        part = tuple(slice(None) if n in done else v for n, v in (("y", p.y), ("x", p.x), ("c", p.c)))
        view = self.buf.at[part] if self.flat else self.buf.at[(slice(None),) + part]
        slot = (0 if self.flat else p.dpn - 2) + stage
        return [remote(view, view, self.send.at[slot], self.recv.at[slot], p.across(axis))]

    def start(self, stage):
        for copy in self.copies(stage):
            copy.start()

    def step(self, stage):
        for copy in self.copies(stage):
            copy.wait_recv()
        if stage + 1 < len(self.order):
            self.start(stage + 1)

    def drain(self):
        for stage in range(len(self.order)):
            for copy in self.copies(stage):
                copy.wait_send()


class Scatter:
    def __init__(self, place, acc, recvs, send, recv, order):
        self.place, self.acc, self.recvs, self.send, self.recv = place, acc, recvs, send, recv
        self.order = order + ("z",)

    def view(self, stage, other):
        p = self.place
        done = self.order[:stage]
        here = {"y": p.y, "x": p.x, "c": p.c}
        part = []
        for name in ("y", "x", "c"):
            if name == self.order[stage]:
                part.append(1 - here[name] if other else here[name])
            elif name in done:
                part.append(here[name])
            else:
                part.append(slice(None))
        return (slice(None),) + tuple(part)

    def copies(self, stage):
        p = self.place
        if stage == 3:
            rest = (p.y, p.x, p.c)
            return [
                remote(
                    self.acc.at[((p.dp + k + 1) % p.dpn,) + rest],
                    self.recvs[3].at[k],
                    self.send.at[3 + k],
                    self.recv.at[3 + k],
                    p.along(k + 1),
                )
                for k in range(p.dpn - 1)
            ]
        return [
            remote(
                self.acc.at[self.view(stage, True)],
                self.recvs[stage],
                self.send.at[stage],
                self.recv.at[stage],
                p.across(self.order[stage]),
            )
        ]

    def start(self, stage):
        for copy in self.copies(stage):
            copy.start()

    def step(self, stage):
        for copy in self.copies(stage):
            copy.wait_recv()
        where = self.view(stage, False)
        self.acc[where] = self.acc[where] + self.recvs[stage][...]
        self.start(stage + 1)

    def total(self):
        p = self.place
        for copy in self.copies(3):
            copy.wait_recv()
        result = self.acc[p.dp, p.y, p.x, p.c].astype(f32)
        for k in range(p.dpn - 1):
            result = result + self.recvs[3][k].astype(f32)
        return result

    def drain(self):
        for stage in range(4):
            for copy in self.copies(stage):
                copy.wait_send()


def heads_of(value):
    return value.reshape(HEADS, HD, value.shape[-1])


def per_head(value):
    return jnp.sum(heads_of(value), axis=1)


def spread(rows):
    return jnp.broadcast_to(rows[:, None, :], (HEADS, HD, rows.shape[-1])).reshape(D, rows.shape[-1])


def norm_scale(value):
    return lax.rsqrt(jnp.mean(value * value, axis=0, keepdims=True) + epsilon)


def norm_back(grad, normed, scale):
    return scale * (grad - normed * jnp.mean(grad * normed, axis=0, keepdims=True))


def one_head(pair, e):
    row = lax.broadcasted_iota(jnp.int32, pair.shape, 0)
    return jnp.where((row >= HD) == (e == 1), pair, jnp.zeros_like(pair))


def layer(dpn, *refs):
    (tok, pre, nbr, tab, gains, wq, wk, wv, wo, wi, wu, cot) = refs[:12]
    (out, ig, gq, gk, gv, go_, gi, gu, gg) = refs[12:21]
    (
        bufA, bufB, bufO, bufI, bufU, bufT, tokP, stage, xT, coT, niO, niP, qs, kvO, kvP, loc, near,
        nw, gate, lse, dlt, mid, bld, fi, y, gm, bias, G3, Gp, accQ, hgR,
        rI0, rI1, rI2, rI3, rU0, rU1, rU2, rU3, rO0, rO1, rO2, rO3, rQ0, rQ1, rQ2, rQ3,
        ags, agr, rss, rsr, hs, hr, dms,
    ) = refs[21:]
    place = Place(dpn)
    dp, s = place.dp, place.s
    cy, cx, cc = place.y, place.x, place.c
    nseq = 8
    nxt = (dp, (s + 1) % nseq)
    prv = (dp, (s + nseq - 1) % nseq)

    tok_in = [pltpu.make_async_copy(tok.at[b], stage.at[b], dms.at[b]) for b in range(NB)]
    for copy in tok_in:
        copy.start()
    for p in range(PAIRS):
        to = bufA if p < 2 else bufB
        for i, w in enumerate((wq, wk, wv)):
            at = (p % 2) * 384 + i * 128
            to[dp, cy, cx, cc, :, at : at + 128] = w[:, p * 128 : (p + 1) * 128]
    bufA[dp, cy, cx, cc, :, 768:896] = gains[...]
    bufO[dp, cy, cx, cc, :, 0:512] = wo[...]
    bufO[dp, cy, cx, cc, :, 512:640] = gains[...]
    bufI[dp, cy, cx, cc] = wi[...]
    bufU[dp, cy, cx, cc] = wu[...]
    bufT[cy, cx, cc] = tab[...]

    barrier = pltpu.get_barrier_semaphore()
    greet = [place.along(k + 1) for k in range(dpn - 1)]
    greet += [place.across("y"), place.across("x"), place.across("c"), nxt, prv]
    for device in greet:
        pl.semaphore_signal(barrier, inc=1, device_id=device, device_id_type=MESH)
    pl.semaphore_wait(barrier, len(greet))

    ag = [
        Gather(place, bufA, ags.at[0], agr.at[0], ("y", "x", "c")),
        Gather(place, bufB, ags.at[1], agr.at[1], ("x", "y", "c")),
        Gather(place, bufT, ags.at[2], agr.at[2], ("y", "x", "c"), flat=True),
        Gather(place, bufO, ags.at[3], agr.at[3], ("x", "y", "c")),
        Gather(place, bufI, ags.at[4], agr.at[4], ("y", "x", "c")),
        Gather(place, bufU, ags.at[5], agr.at[5], ("x", "y", "c")),
    ]
    A, B, T, O, I, U = ag
    halo = [remote(tok.at[b], tokP.at[b], hs.at[b], hr.at[b], nxt) for b in range(NB)]
    back = [remote(tokP.at[b], hgR.at[b], hs.at[2 + b], hr.at[2 + b], prv) for b in range(NB)]

    A.start(0)
    B.start(0)
    halo[0].start()

    seg = s
    base = seg * SEG
    away = (seg == 0).astype(f32) * far

    def set_bias(b):
        q = lax.broadcasted_iota(jnp.int32, (1, SEG), 1)
        k = lax.broadcasted_iota(jnp.int32, (SEG, SEG), 0)
        limit = jnp.where(base + q < pre[b], jnp.maximum(q, pre[b] - 1 - base), q)
        bias[b] = jnp.where(k <= limit, 0.0, -far).astype(f32)

    for copy in tok_in:
        copy.wait()
    for b in range(NB):
        xT[b] = stage[b].T
    cot_in = [pltpu.make_async_copy(cot.at[b], stage.at[b], dms.at[b]) for b in range(NB)]
    for copy in cot_in:
        copy.start()
    A.step(0)
    B.step(0)
    halo[1].start()
    T.start(0)
    for b in range(NB):
        set_bias(b)
    A.step(1)
    B.step(1)
    O.start(0)
    for copy in cot_in:
        copy.wait()
    for b in range(NB):
        coT[b] = stage[b].T
    A.step(2)
    B.step(2)
    I.start(0)
    U.start(0)
    A.step(3)
    B.step(3)
    T.step(0)
    O.step(0)

    again = bufA[..., 768:896].reshape(D, 128)[:, 0:1].astype(f32)

    def w3(p):
        at = (p % 2) * 384
        return (bufA if p < 2 else bufB)[..., at : at + 384].reshape(D, 384)

    def own_proj(b):
        X = xT[b].astype(f32)
        niO[b] = (X * norm_scale(X) * again).astype(bf16)
        for p in range(PAIRS):
            w = w3(p)
            kvO[b, p] = mm(niO[b], w[:, 128:384], 0, 0).astype(bf16)
            qs[b, p] = mm(w[:, 0:128], niO[b], 0, 0).astype(bf16) * jnp.asarray(0.125, bf16)

    def prev_proj(b):
        X = tokP[b].T.astype(f32)
        niP[b] = (X * norm_scale(X) * again).astype(bf16)
        for p in range(PAIRS):
            kvP[b, p] = mm(niP[b], w3(p)[:, 128:384], 0, 0).astype(bf16)

    def attend(b, p):
        kp, vp = kvP[b, p, :, 0:128], kvP[b, p, :, 128:256].T
        ko, vo = kvO[b, p, :, 0:128], kvO[b, p, :, 128:256].T
        q2 = qs[b, p]
        for e in range(2):
            qz = one_head(q2, e)
            sp = mm(kp, qz, 1, 0)
            so = mm(ko, qz, 1, 0) + bias[b]
            top = jnp.maximum(
                jnp.max(so, axis=0, keepdims=True), jnp.max(sp, axis=0, keepdims=True) - away
            )
            ep = jnp.exp(sp - (top + away))
            eo = jnp.exp(so - top)
            total = jnp.sum(ep, axis=0, keepdims=True) + jnp.sum(eo, axis=0, keepdims=True)
            rows = slice(e * HD, (e + 1) * HD)
            o = mm(vp[rows], ep.astype(bf16), 1, 0) + mm(vo[rows], eo.astype(bf16), 1, 0)
            loc[b, p, rows] = o / total
            lse[b, 2 * p + e] = top + jnp.log(total)

    def attend_loop(b, lo, hi):
        def body(p, carry):
            attend(b, p)
            return carry

        lax.fori_loop(lo, hi, body, 0)

    def remember(b):
        table = bufT[...].reshape(-1, D)
        q = qs[b].reshape(D, SEG).astype(f32)
        row = lax.broadcasted_iota(jnp.int32, (table.shape[0], SEG), 0)
        scores = []
        for k in range(KNN):
            hot = (row == nbr[b, k : k + 1, :]).astype(bf16)
            rows = mm(table, hot, 0, 0)
            near[b, k] = rows.astype(bf16)
            scores.append(per_head(q * rows))
        top = scores[0]
        for k in range(1, KNN):
            top = jnp.maximum(top, scores[k])
        scores = [jnp.exp(v - top) for v in scores]
        total = scores[0] + scores[1] + scores[2] + scores[3]
        for k in range(KNN):
            nw[b, k] = scores[k] / total

    def blend(b):
        cols = bufO[..., 512:640].reshape(D, 128).astype(f32)
        gvec, fgain = cols[:, 1:2], cols[:, 2:3]
        recalled = spread(nw[b, 0]) * near[b, 0].astype(f32)
        for k in range(1, KNN):
            recalled = recalled + spread(nw[b, k]) * near[b, k].astype(f32)
        local = loc[b].reshape(D, SEG)
        opened = jax.nn.sigmoid(per_head(local * gvec))
        gate[b] = opened
        wide = spread(opened)
        blended = (wide * recalled + (1.0 - wide) * local).astype(bf16)
        bld[b] = blended
        w = bufO[..., 0:512].reshape(D, D)
        middle = xT[b].astype(f32) + mm(w, blended, 0, 0)
        mid[b] = middle
        y[b] = middle
        fi[b] = (middle * norm_scale(middle) * fgain).astype(bf16)

    for b in range(NB):
        own_proj(b)
        if b == 0:
            T.step(1)
            O.step(1)
    halo[0].wait_recv()
    prev_proj(0)
    T.step(2)
    O.step(2)
    I.step(0)
    U.step(0)
    attend_loop(0, 0, 2)
    halo[1].wait_recv()
    prev_proj(1)
    O.step(3)
    attend_loop(0, 2, 4)
    remember(0)
    blend(0)
    I.step(1)
    U.step(1)
    attend_loop(1, 0, 2)
    I.step(2)
    U.step(2)
    attend_loop(1, 2, 4)
    remember(1)
    blend(1)
    I.step(3)
    U.step(3)
    for g in ag:
        g.drain()
    for copy in halo:
        copy.wait_send()

    root = 0.7978845608028654
    RI = Scatter(place, bufI, (rI0, rI1, rI2, rI3), rss.at[0], rsr.at[0], ("c", "x", "y"))
    RU = Scatter(place, bufU, (rU0, rU1, rU2, rU3), rss.at[1], rsr.at[1], ("c", "y", "x"))
    RO = Scatter(place, bufO, (rO0, rO1, rO2, rO3), rss.at[2], rsr.at[2], ("c", "x", "y"))
    RQ = [
        Scatter(
            place,
            accQ.at[p],
            (rQ0.at[p], rQ1.at[p], rQ2.at[p], rQ3.at[p]),
            rss.at[3 + p],
            rsr.at[3 + p],
            ("c", "x", "y") if p % 2 else ("c", "y", "x"),
        )
        for p in range(PAIRS)
    ]

    for j in range(4):
        lanes = slice(j * 512, (j + 1) * 512)
        win = bufI[..., lanes].reshape(D, 512)
        wout = bufU[j].reshape(512, D)
        gin = None
        for b in range(NB):
            v = mm(win, fi[b], 0, 0)
            gh = mm(wout, coT[b], 1, 0)
            v2 = v * v
            t = jnp.tanh(root * v * (1.0 + 0.044715 * v2))
            half = 0.5 * (1.0 + t)
            hb = (v * half).astype(bf16)
            slope = half + 0.5 * v * (1.0 - t * t) * (root * (1.0 + 3 * 0.044715 * v2))
            gp = (gh * slope).astype(bf16)
            y[b] = y[b] + mm(wout, hb, 0, 0)
            back_in = mm(win, gp, 1, 0)
            if j == 0:
                gm[b] = back_in
            else:
                gm[b] = gm[b] + back_in
            a = mm(hb, coT[b], 1, 1)
            c = mm(fi[b], gp, 1, 1)
            if b == 0:
                gout, gin = a, c
            else:
                gout, gin = gout + a, gin + c
        bufU[j] = gout.astype(bf16).reshape(2, 2, 2, 64, D)
        bufI[..., lanes] = gin.astype(bf16).reshape(dpn, 2, 2, 2, 16, 512)
    RI.start(0)
    RU.start(0)

    out_copies = []
    cols = bufO[..., 512:640].reshape(D, 128).astype(f32)
    gvec, fgain = cols[:, 1:2], cols[:, 2:3]
    wout_a = bufO[..., 0:512].reshape(D, D)
    gwo = None
    ggv = None
    for b in range(NB):
        stage[b] = y[b].astype(bf16).T
        copy = pltpu.make_async_copy(stage.at[b], out.at[b], dms.at[b])
        copy.start()
        out_copies.append(copy)
        middle = mid[b]
        scale = norm_scale(middle)
        grad = coT[b].astype(f32) + norm_back(gm[b] * fgain, middle * scale, scale)
        gm[b] = grad
        gb = grad.astype(bf16)
        part = mm(bld[b], gb, 1, 1)
        gwo = part if gwo is None else gwo + part
        gbl = mm(wout_a, gb, 1, 0)
        local = loc[b].reshape(D, SEG)
        opened = gate[b]
        along = per_head(gbl * local)
        hits = [per_head(gbl * near[b, k].astype(f32)) for k in range(KNN)]
        mixed = hits[0] * nw[b, 0]
        for k in range(1, KNN):
            mixed = mixed + hits[k] * nw[b, k]
        ggate = (mixed - along) * opened * (1.0 - opened)
        wide = spread(ggate)
        part = jnp.sum(wide * local, axis=1, keepdims=True)
        ggv = part if ggv is None else ggv + part
        dlo = (spread(1.0 - opened) * gbl + wide * gvec).astype(bf16)
        fi[b] = dlo
        dots = per_head(dlo.astype(f32) * local)
        for h in range(HEADS):
            dlt[b, h] = dots[h : h + 1, :]
        dq = None
        for k in range(KNN):
            weight = spread(nw[b, k] * opened * (hits[k] - mixed) * 0.125)
            part = weight * near[b, k].astype(f32)
            dq = part if dq is None else dq + part
        y[b] = dq
    bufO[..., 0:512] = gwo.astype(bf16).reshape(dpn, 2, 2, 2, 16, 512)
    bufO[..., 512:640] = jnp.broadcast_to(ggv, (D, 128)).astype(bf16).reshape(dpn, 2, 2, 2, 16, 128)
    RO.start(0)

    def retreat(b, p, kv, own):
        k2, v2 = kv[b, p, :, 0:128], kv[b, p, :, 128:256]
        kt = k2.T
        q2 = qs[b, p]
        d2 = fi[b, pl.ds(p * 128, 128), :]
        for e in range(2):
            rows = slice(e * HD, (e + 1) * HD)
            sc = mm(k2, one_head(q2, e), 1, 0)
            if own:
                pr = jnp.exp((sc + bias[b]) - lse[b, 2 * p + e])
            else:
                pr = jnp.exp(sc - (lse[b, 2 * p + e] + away))
            dpr = mm(v2, one_head(d2, e), 1, 0)
            ds = (pr * (dpr - dlt[b, 2 * p + e])).astype(bf16)
            dv = mm(d2[rows], pr.astype(bf16), 1, 1).astype(bf16)
            dk = mm(q2[rows], ds, 1, 1).astype(bf16)
            dq = mm(kt[rows], ds, 1, 0) * 0.125
            at = pl.ds(p * 128 + e * HD, HD)
            if own:
                G3[b, p, e * HD : (e + 1) * HD] = (y[b, at, :] + dq).astype(bf16)
                G3[b, p, 128 + e * HD : 128 + (e + 1) * HD] = dk
                G3[b, p, 256 + e * HD : 256 + (e + 1) * HD] = dv
            else:
                y[b, at, :] = y[b, at, :] + dq
                Gp[b, p, e * HD : (e + 1) * HD] = dk
                Gp[b, p, 128 + e * HD : 128 + (e + 1) * HD] = dv

    for b in range(NB):

        def body(p, carry):
            retreat(b, p, kvP, False)
            return carry

        lax.fori_loop(0, PAIRS, body, 0)
        sent = mm(w3(0)[:, 128:384], Gp[b, 0], 1, 0)
        for p in range(1, PAIRS):
            sent = sent + mm(w3(p)[:, 128:384], Gp[b, p], 1, 0)
        tokP[b] = sent.astype(bf16)
        back[b].start()
        if b == 0:
            RI.step(0)
            RU.step(0)
            RO.step(0)
        else:
            RI.step(1)
            RU.step(1)
            RO.step(1)

    for p in range(PAIRS):

        def body(b, carry):
            retreat(b, p, kvO, True)
            return carry

        body(0,0);body(1,0)
        quer = mm(niO[0], G3[0, p, 0:128], 1, 1) + mm(niO[1], G3[1, p, 0:128], 1, 1)
        accQ[p, ..., 0:128] = quer.astype(bf16).reshape(dpn, 2, 2, 2, 16, 128)
        rest = mm(niO[0], G3[0, p, 128:384], 1, 1)
        rest = rest + mm(niP[0], Gp[0, p], 1, 1)
        rest = rest + mm(niO[1], G3[1, p, 128:384], 1, 1)
        rest = rest + mm(niP[1], Gp[1, p], 1, 1)
        accQ[p, ..., 128:384] = rest.astype(bf16).reshape(dpn, 2, 2, 2, 16, 256)
        RQ[p].start(0)
        if p == 0:
            RI.step(2)
            RU.step(2)
            RO.step(2)
        if p == 1:
            RQ[0].step(0)
            gi[...] = RI.total()
            gu[...] = RU.total()
            last = RO.total()
        if p == 2:
            RQ[0].step(1)
            RQ[1].step(0)
        if p == 3:
            RQ[0].step(2)
            RQ[1].step(1)
            RQ[2].step(0)

    def finish(b):
        total = mm(w3(0), G3[b, 0], 1, 0)
        for p in range(1, PAIRS):
            total = total + mm(w3(p), G3[b, p], 1, 0)
        total = total + hgR[b].astype(f32)
        X = xT[b].astype(f32)
        scale = norm_scale(X)
        res = gm[b] + norm_back(total * again, X * scale, scale)
        mid[b] = res.T
        copy = pltpu.make_async_copy(mid.at[b], ig.at[b], dms.at[2 + b])
        copy.start()
        return copy

    RQ[3].step(0)
    back[0].wait_recv()
    copy0 = finish(0)
    RQ[1].step(2)
    RQ[2].step(1)
    RQ[3].step(1)
    back[1].wait_recv()
    copy1 = finish(1)
    RQ[2].step(2)
    RQ[3].step(2)
    go_[...] = last[:, 0:512]
    own = gains[...].astype(f32)
    fsum = jnp.sum(gi[...] * wi[...].astype(f32), axis=1, keepdims=True) / own[:, 2:3]
    for p in range(PAIRS):
        res = RQ[p].total()
        gq[:, p * 128 : (p + 1) * 128] = res[:, 0:128]
        gk[:, p * 128 : (p + 1) * 128] = res[:, 128:256]
        gv[:, p * 128 : (p + 1) * 128] = res[:, 256:384]
    asum = (
        gq[...] * wq[...].astype(f32) + gk[...] * wk[...].astype(f32) + gv[...] * wv[...].astype(f32)
    )
    asum = jnp.sum(asum, axis=1, keepdims=True) / own[:, 0:1]
    lane = lax.broadcasted_iota(jnp.int32, (16, 128), 1)
    gg[...] = jnp.where(lane == 0, asum, jnp.where(lane == 1, last[:, 513:514], fsum))
    for r in [RI, RU, RO] + RQ:
        r.drain()
    for copy in back:
        copy.wait_send()
    for copy in out_copies + [copy0, copy1]:
        copy.wait()


def fused(dpn, tokens, prefix, neighbours, table, attn_gain, w_query, w_key, w_value, gate_vector,
          w_output, ffn_gain, w_inner, w_outer, cotangent):
    gains = jnp.pad(jnp.stack([attn_gain, gate_vector, ffn_gain], axis=1), ((0, 0), (0, 125)))
    vm = pl.BlockSpec(memory_space=pltpu.VMEM)
    hb = pl.BlockSpec(memory_space=pl.ANY)
    sm = pl.BlockSpec(memory_space=pltpu.SMEM)
    V = pltpu.VMEM
    lead = (dpn, 2, 2, 2)
    sq = (NB, D, SEG)

    def recvs(rows, cols, pre=()):
        return [
            V(pre + (dpn, 2, 2, rows, cols), bf16),
            V(pre + (dpn, 2, rows, cols), bf16),
            V(pre + (dpn, rows, cols), bf16),
            V(pre + (dpn - 1, rows, cols), bf16),
        ]

    scratch = [
        V(lead + (16, 896), bf16),
        V(lead + (16, 768), bf16),
        V(lead + (16, 640), bf16),
        V(lead + (16, FF), bf16),
        V(lead + (64, D), bf16),
        V((2, 2, 2) + table.shape, bf16),
        V(sq, bf16),
        V(sq, bf16),
        V(sq, bf16),
        V(sq, bf16),
        V(sq, bf16),
        V(sq, bf16),
        V((NB, PAIRS, 128, SEG), bf16),
        V((NB, PAIRS, SEG, 256), bf16),
        V((NB, PAIRS, SEG, 256), bf16),
        V((NB, PAIRS, 128, SEG), f32),
        V((NB, KNN, D, SEG), bf16),
        V((NB, KNN, HEADS, SEG), f32),
        V((NB, HEADS, SEG), f32),
        V((NB, HEADS, 1, SEG), f32),
        V((NB, HEADS, 1, SEG), f32),
        V(sq, f32),
        V(sq, bf16),
        V(sq, bf16),
        V(sq, f32),
        V(sq, f32),
        V((NB, SEG, SEG), f32),
        V((NB, PAIRS, 384, SEG), bf16),
        V((NB, PAIRS, 256, SEG), bf16),
        V((PAIRS,) + lead + (16, 384), bf16),
        V(sq, bf16),
    ]
    scratch += recvs(16, FF) + recvs(64, D) + recvs(16, 640) + recvs(16, 384, (PAIRS,))
    dma = pltpu.SemaphoreType.DMA
    scratch += [
        dma((6, dpn + 2)), dma((6, dpn + 2)), dma((7, dpn + 2)), dma((7, dpn + 2)), dma((4,)), dma((4,)), dma((4,)),
    ]
    rows = w_query.shape[0]
    sds = jax.ShapeDtypeStruct
    out = pl.pallas_call(
        lambda *refs: layer(dpn, *refs),
        name="layer",
        out_shape=(
            sds(tokens.shape, bf16),
            sds(tokens.shape, f32),
            sds((rows, D), f32),
            sds((rows, D), f32),
            sds((rows, D), f32),
            sds((rows, D), f32),
            sds((rows, FF), f32),
            sds(w_outer.shape, f32),
            sds((rows, 128), f32),
        ),
        in_specs=[hb, sm, vm, vm, vm, vm, vm, vm, vm, vm, vm, hb],
        out_specs=(hb, hb) + (vm,) * 7,
        scratch_shapes=scratch,
        compiler_params=pltpu.CompilerParams(
            collective_id=0, has_side_effects=True, vmem_limit_bytes=63 * 2**20
        ),
    )(
        tokens, prefix, neighbours.transpose(0, 2, 1), table, gains, w_query, w_key, w_value, w_output,
        w_inner, w_outer, cotangent,
    )
    return (
        out[0], out[1], out[8][:, 0], out[2], out[3], out[4], out[8][:, 1], out[5], out[8][:, 2], out[6], out[7],
    )


masked_floor = -1000000000.0


def from_behind(value, axis, by):
    count = lax.axis_size(axis)
    pairs = [(i, i + by) for i in range(count) if 0 <= i + by < count]
    return lax.ppermute(value, axis, pairs)


def times_plain(left, right):
    return jnp.dot(left, right, preferred_element_type=jnp.float32)


def times_first_t(left, right):
    return lax.dot_general(
        left, right, (((0,), (0,)), ((), ())), preferred_element_type=jnp.float32
    )


def times_second_t(left, right):
    return lax.dot_general(
        left, right, (((1,), (1,)), ((), ())), preferred_element_type=jnp.float32
    )


def gelu_tanh(values):
    return jax.nn.gelu(values, approximate=True)


def rms_scale(values):
    return lax.rsqrt(jnp.mean(values * values, axis=-1, keepdims=True) + epsilon)


def norm_back_rows(grad_normed, normed, scale):
    return scale * (grad_normed - normed * jnp.mean(grad_normed * normed, axis=-1, keepdims=True))


def split_heads(rows):
    return rows.reshape(rows.shape[0], HEADS, HD).transpose(1, 0, 2)


def merge_heads(stacked):
    return stacked.transpose(1, 0, 2).reshape(stacked.shape[1], D)


def visible_mask(segment, prefix_len):
    query_pos = segment * SEG + lax.iota(jnp.int32, SEG)
    key_pos = (segment - 1) * SEG + lax.iota(jnp.int32, 2 * SEG)
    return (key_pos[None, :] >= 0) & (
        (key_pos[None, :] <= query_pos[:, None])
        | (query_pos[:, None] < prefix_len) & (key_pos[None, :] < prefix_len)
    )


def fetch_attention(attn_gain, w_query, w_key, w_value, gate_vector, w_output):
    return (
        lax.all_gather(attn_gain, ("dp", "seq"), axis=0, tiled=True),
        lax.all_gather(w_query, ("dp", "seq"), axis=0, tiled=True),
        lax.all_gather(w_key, ("dp", "seq"), axis=0, tiled=True),
        lax.all_gather(w_value, ("dp", "seq"), axis=0, tiled=True),
        lax.all_gather(gate_vector, ("dp", "seq"), axis=0, tiled=True),
        lax.all_gather(w_output, ("dp", "seq"), axis=0, tiled=True),
    )


def fetch_feedforward(ffn_gain, w_inner, w_outer):
    return (
        lax.all_gather(ffn_gain, ("dp", "seq"), axis=0, tiled=True),
        lax.all_gather(w_inner, ("dp", "seq"), axis=0, tiled=True),
        lax.all_gather(w_outer, ("dp", "seq"), axis=0, tiled=True),
    )


def forward_pass(tokens_row, visible, near_b, attn_set, ffn_set):
    attn_gain, w_query, w_key, w_value, gate_vector, w_output = attn_set
    ffn_gain, w_inner, w_outer = ffn_set
    rows_count = tokens_row.shape[0]
    inputs_f = tokens_row.astype(jnp.float32)
    scale_one = rms_scale(inputs_f)
    normed_one = inputs_f * scale_one
    normed_in = (normed_one * attn_gain.astype(jnp.float32)).astype(jnp.bfloat16)
    query_b = times_plain(normed_in, w_query).astype(jnp.bfloat16)
    key_b = times_plain(normed_in, w_key).astype(jnp.bfloat16)
    value_b = times_plain(normed_in, w_value).astype(jnp.bfloat16)
    key_prev, value_prev = from_behind((key_b, value_b), "seq", 1)
    key_all = jnp.concatenate([key_prev, key_b], axis=0)
    value_all = jnp.concatenate([value_prev, value_b], axis=0)
    visible_f = visible.astype(jnp.float32)

    def head_forward(operands):
        query_h, key_h, value_h = operands
        scores = jnp.where(visible, times_second_t(query_h, key_h) * 0.125, masked_floor)
        row_max = jnp.max(scores, axis=1, keepdims=True)
        exponent = jnp.exp(scores - row_max) * visible_f
        row_sum = jnp.sum(exponent, axis=1, keepdims=True)
        attn_probs = (exponent / row_sum).astype(jnp.bfloat16)
        return (times_plain(attn_probs, value_h), (row_max + jnp.log(row_sum))[:, 0])

    local_h, log_norm = lax.map(
        head_forward, (split_heads(query_b), split_heads(key_all), split_heads(value_all))
    )
    local_t = local_h.transpose(1, 0, 2)
    query_t = query_b.reshape(rows_count, HEADS, HD)
    near_scores = (
        jnp.einsum("shd,skhd->shk", query_t, near_b, preferred_element_type=jnp.float32) * 0.125
    )
    near_exp = jnp.exp(near_scores - jnp.max(near_scores, axis=-1, keepdims=True))
    near_weights = near_exp / jnp.sum(near_exp, axis=-1, keepdims=True)
    recalled = jnp.einsum("shk,skhd->shd", near_weights, near_b, preferred_element_type=jnp.float32)
    gate_h = gate_vector.astype(jnp.float32).reshape(HEADS, HD)
    gate_open = jax.nn.sigmoid(jnp.sum(local_t * gate_h, axis=-1, keepdims=True))
    blended_b = (
        (gate_open * recalled + (1.0 - gate_open) * local_t)
        .reshape(rows_count, D)
        .astype(jnp.bfloat16)
    )
    middle = inputs_f + times_plain(blended_b, w_output)
    scale_two = rms_scale(middle)
    normed_two = middle * scale_two
    ffn_in = (normed_two * ffn_gain.astype(jnp.float32)).astype(jnp.bfloat16)
    hidden_pre = times_plain(ffn_in, w_inner)
    hidden_b = gelu_tanh(hidden_pre).astype(jnp.bfloat16)
    result = (middle + times_plain(hidden_b, w_outer)).astype(jnp.bfloat16)
    kept = (
        scale_one,
        normed_one,
        normed_in,
        query_b,
        key_all,
        value_all,
        log_norm,
        local_t,
        near_weights,
        recalled,
        gate_open,
        blended_b,
        scale_two,
        normed_two,
        ffn_in,
        hidden_pre,
        hidden_b,
    )
    return (result, kept)


def backward_pass(kept, cot_row, visible, near_b, attn_set, ffn_set):
    (
        scale_one,
        normed_one,
        normed_in,
        query_b,
        key_all,
        value_all,
        log_norm,
        local_t,
        near_weights,
        recalled,
        gate_open,
        blended_b,
        scale_two,
        normed_two,
        ffn_in,
        hidden_pre,
        hidden_b,
    ) = kept
    attn_gain, w_query, w_key, w_value, gate_vector, w_output = attn_set
    ffn_gain, w_inner, w_outer = ffn_set
    rows_count = cot_row.shape[0]
    dout = cot_row.astype(jnp.float32)
    grad_outer = times_first_t(hidden_b, cot_row)
    grad_hidden = times_second_t(cot_row, w_outer)
    unused_value, gelu_pull = jax.vjp(gelu_tanh, hidden_pre)
    grad_pre = gelu_pull(grad_hidden)[0].astype(jnp.bfloat16)
    grad_inner = times_first_t(ffn_in, grad_pre)
    grad_ffn_in = times_second_t(grad_pre, w_inner)
    grad_ffn_gain = jnp.sum(grad_ffn_in * normed_two, axis=0)
    grad_middle = dout + norm_back_rows(
        grad_ffn_in * ffn_gain.astype(jnp.float32), normed_two, scale_two
    )
    grad_branch_b = grad_middle.astype(jnp.bfloat16)
    grad_output = times_first_t(blended_b, grad_branch_b)
    grad_blended = times_second_t(grad_branch_b, w_output).reshape(rows_count, HEADS, HD)
    gate_h = gate_vector.astype(jnp.float32).reshape(HEADS, HD)
    grad_recalled = gate_open * grad_blended
    grad_gate = (
        jnp.sum(grad_blended * (recalled - local_t), axis=-1, keepdims=True)
        * gate_open
        * (1.0 - gate_open)
    )
    grad_gate_vector = jnp.sum(grad_gate * local_t, axis=0).reshape(D)
    grad_local_b = (
        ((1.0 - gate_open) * grad_blended + grad_gate * gate_h)
        .astype(jnp.bfloat16)
        .transpose(1, 0, 2)
    )
    grad_near_w = jnp.einsum(
        "shd,skhd->shk", grad_recalled, near_b, preferred_element_type=jnp.float32
    )
    grad_near = near_weights * (
        grad_near_w - jnp.sum(near_weights * grad_near_w, axis=-1, keepdims=True)
    )
    grad_query_near = (
        jnp.einsum("shk,skhd->shd", grad_near, near_b, preferred_element_type=jnp.float32) * 0.125
    )
    visible_f = visible.astype(jnp.float32)

    def head_backward(operands):
        query_h, key_h, value_h, grad_h, norm_h = operands
        scores = jnp.where(visible, times_second_t(query_h, key_h) * 0.125, masked_floor)
        attn_probs = jnp.exp(scores - norm_h[:, None]) * visible_f
        grad_probs = times_second_t(grad_h, value_h)
        grad_scores = (
            attn_probs * (grad_probs - jnp.sum(attn_probs * grad_probs, axis=1, keepdims=True))
        ).astype(jnp.bfloat16)
        return (
            times_plain(grad_scores, key_h) * 0.125,
            times_first_t(grad_scores, query_h) * 0.125,
            times_first_t(attn_probs.astype(jnp.bfloat16), grad_h),
        )

    grad_query_h, grad_key_h, grad_value_h = lax.map(
        head_backward,
        (
            split_heads(query_b),
            split_heads(key_all),
            split_heads(value_all),
            grad_local_b,
            log_norm,
        ),
    )
    grad_key_all = merge_heads(grad_key_h)
    grad_value_all = merge_heads(grad_value_h)
    later_key, later_value = (
        from_behind(grad_key_all[:rows_count].astype(jnp.bfloat16), "seq", -1).astype(jnp.float32),
        from_behind(grad_value_all[:rows_count].astype(jnp.bfloat16), "seq", -1).astype(
            jnp.float32
        ),
    )
    grad_query_b = (merge_heads(grad_query_h) + grad_query_near.reshape(rows_count, D)).astype(
        jnp.bfloat16
    )
    grad_key_b = (grad_key_all[rows_count:] + later_key).astype(jnp.bfloat16)
    grad_value_b = (grad_value_all[rows_count:] + later_value).astype(jnp.bfloat16)
    grad_query = times_first_t(normed_in, grad_query_b)
    grad_key = times_first_t(normed_in, grad_key_b)
    grad_value = times_first_t(normed_in, grad_value_b)
    grad_normed_in = (
        times_second_t(grad_query_b, w_query)
        + times_second_t(grad_key_b, w_key)
        + times_second_t(grad_value_b, w_value)
    )
    grad_attn_gain = jnp.sum(grad_normed_in * normed_one, axis=0)
    input_grad = grad_middle + norm_back_rows(
        grad_normed_in * attn_gain.astype(jnp.float32), normed_one, scale_one
    )
    grads = (
        grad_attn_gain,
        grad_query,
        grad_key,
        grad_value,
        grad_gate_vector,
        grad_output,
        grad_ffn_gain,
        grad_inner,
        grad_outer,
    )
    return (grads, input_grad)


def plain(
    tokens,
    prefix,
    neighbours,
    table,
    attn_gain,
    w_query,
    w_key,
    w_value,
    gate_vector,
    w_output,
    ffn_gain,
    w_inner,
    w_outer,
    cotangent,
):
    full_table = lax.all_gather(table, "seq", axis=0, tiled=True)
    segment = lax.axis_index("seq")
    rows_count = tokens.shape[1]
    outputs = []
    input_grads = []
    running = ()
    for micro_batch in range(tokens.shape[0]):
        visible = visible_mask(segment, prefix[micro_batch])
        near_b = jnp.take(full_table, neighbours[micro_batch].reshape(-1), axis=0).reshape(
            rows_count, KNN, HEADS, HD
        )
        attn_fwd = fetch_attention(attn_gain, w_query, w_key, w_value, gate_vector, w_output)
        ffn_fwd = fetch_feedforward(ffn_gain, w_inner, w_outer)
        result, kept = forward_pass(tokens[micro_batch], visible, near_b, attn_fwd, ffn_fwd)
        attn_back = fetch_attention(attn_gain, w_query, w_key, w_value, gate_vector, w_output)
        ffn_back = fetch_feedforward(ffn_gain, w_inner, w_outer)
        grads, input_grad = backward_pass(
            kept, cotangent[micro_batch], visible, near_b, attn_back, ffn_back
        )
        if micro_batch == 0:
            running = grads
        else:
            running = tuple((earlier + increment for earlier, increment in zip(running, grads)))
        outputs.append(result)
        input_grads.append(input_grad)
    shares = lax.psum_scatter(running, ("dp", "seq"), scatter_dimension=0, tiled=True)
    return (
        jnp.stack(outputs),
        jnp.stack(input_grads),
        shares[0],
        shares[1],
        shares[2],
        shares[3],
        shares[4],
        shares[5],
        shares[6],
        shares[7],
        shares[8],
    )


def solution(mesh):
    dpn = mesh.shape["dp"]

    def local(*args):
        if mesh.shape["seq"] == 8 and args[5].shape[0] == 16:
            return fused(dpn, *args)
        return plain(*args)

    rows = P(("dp", "seq"))
    wide = P(("dp", "seq"), None)
    block = P("dp", "seq", None)
    return jax.shard_map(
        local,
        mesh=mesh,
        in_specs=(
            block, P("dp"), block, P("seq", None), rows, wide, wide, wide, rows, wide, rows, wide, wide, block,
        ),
        out_specs=(block, block, rows, wide, wide, wide, rows, wide, rows, wide, wide),
        check_vma=False,
    )
```

```python
import jax
import jax.numpy as jnp
from jax import lax
from jax.experimental import pallas as pl
from jax.experimental.pallas import tpu as pltpu
from jax.sharding import PartitionSpec as P

D = 512
HEADS = 8
HD = 64
KNN = 4
SEG = 512
FF = 2048
PAIRS = 4
NB = 2
MESH = pl.DeviceIdType.MESH

epsilon = 1e-06
far = 1e30
f32 = jnp.float32
bf16 = jnp.bfloat16


def mm(left, right, over_left, over_right):
    return lax.dot_general(
        left, right, (((over_left,), (over_right,)), ((), ())), preferred_element_type=f32
    )


(W0, W1, W2, W3, T0, T1, O, U0, U1, I0, I1, I2, I3,
 H0, H1, B0, B1, RI0, RI1, RI2, RI3, RU0, RU1, RO, RQ0, RQ1, RQ2, RQ3) = range(28)
(BEGIN, XT, BIAS, COT, NORM, PROJ, OWN, PN, PP, PREV, REM, BLEND, FFN, GIN, UG, CPRE, GWO, RP, SEND, ROW, DW, FIN, END) = range(23)
Z, Y, X, C = range(4)

GATHERS = (
    (W0, (Z, Y, X, C)),
    (W1, (Y, Z, X, C)),
    (W2, (Z, X, Y, C)),
    (W3, (Y, Z, X, C)),
    (T0, (X, Y, C)),
    (T1, (X, Y, C)),
    (O, (X, Z, Y, C)),
    (U0, (X, Z, Y, C)),
    (U1, (X, Z, Y, C)),
    (I0, (Z, X, Y, C)),
    (I1, (Y, Z, X, C)),
    (I2, (Y, Z, X, C)),
    (I3, (Y, Z, X, C)),
)
SUMS = (
    (RI0, (C, X, Z, Y)),
    (RI1, (C, X, Y, Z)),
    (RI2, (C, Y, Z, X)),
    (RI3, (C, X, Z, Y)),
    (RU0, (C, X, Z, Y)),
    (RU1, (C, Y, Z, X)),
    (RO, (C, Y, X, Z)),
    (RQ0, (C, Y, X, Z)),
    (RQ1, (C, Y, Z, X)),
    (RQ2, (C, X, Y, Z)),
    (RQ3, (C, X, Y, Z)),
)
FORWARD = ((REM, 0), (REM, 1), (PREV, 0), (PREV, 1), (BLEND, 0), (BLEND, 1))
PLAN = {
    (BEGIN,): (W0, W3, O),
    (BIAS, 0): (W1, W2, T0, T1),
    (BIAS, 1): (U1, I1, W3, O),
    (PROJ, 0, 0): (U0,),
    (OWN, 0, 0): (H0, I2, W2, W3, T0, T1, O, I1),
    (OWN, 1, 0): (W1, U0),
    (REM, 0): (H1, I0, I3, O, U0, U1, I1, I2),
    (PP, 0): (O, U1, I0, I1, I3),
    (PREV, 0, 1): (U0, I2),
    (BLEND, 0): (I0, I3),
    (GIN, 2): (RI0, RI1, RI2, I3),
    (RP, 0, 1): (RI3, RU0, RU1, RO, RI0, RI1, RI2),
    (RP, 1, 1): (B0, RI2, RI3, RU0, RU1, RO, RI0, RI1),
    (DW, 2): (B1, RQ0, RQ1, RQ2, RI0, RI1, RI2, RI3, RU0, RU1, RO),
    (DW, 3): (RQ3, RI0, RI2, RQ0, RQ1, RQ2),
}
BEFORE = {
    (NORM, 0): (W0, W1, W2, I1, T0, T1, U1, W0, W2, W3, W0, W1, W0),
    (PROJ, 0, 1): (U1, W2, W3, T0, T1, I2, W1),
    (PN, 0): (H0,),
    (PN, 1): (I2, I0, U0, I3, H1),
    (FFN, 0, 0): (I0,),
    (FIN, 0): (B0,),
    (FIN, 1): (RI1, RO, RQ3, B1),
    (END,): (RI3, RQ2, RQ0, RQ1, RQ3, RI3, RQ2, RQ0, RU0, RU1, RO, RQ3, RQ1, RU0, RU1, RQ2, RQ0, RQ1, RQ3),
}


class Place:
    def __init__(self, dpn):
        self.dpn = dpn
        self.dp = lax.axis_index("dp")
        self.s = lax.axis_index("seq")
        self.c = self.s % 2
        self.x = (self.s // 2) % 2
        self.y = self.s // 4

    def across(self, axis):
        if axis == C:
            return (self.dp, self.s + 1 - 2 * self.c)
        if axis == X:
            return (self.dp, self.s + 2 * (1 - 2 * self.x))
        return (self.dp, self.s + 4 * (1 - 2 * self.y))

    def along(self, step):
        return ((self.dp + step) % self.dpn, self.s)

    def partners(self, axis):
        if axis == Z:
            return [self.along(k + 1) for k in range(self.dpn - 1)]
        return [self.across(axis)]


def remote(src, dst, send, recv, device):
    return pltpu.make_async_remote_copy(
        src_ref=src, dst_ref=dst, send_sem=send, recv_sem=recv, device_id=device, device_id_type=MESH
    )


AXES = (Z, Y, X, C)


class Gather:
    def __init__(self, place, buf, send, recv, order):
        self.place, self.buf, self.send, self.recv, self.order = place, buf, send, recv, order
        self.axes = AXES if Z in order else AXES[1:]
        self.at = 0

    def copies(self, stage):
        p = self.place
        here = {Z: p.dp, Y: p.y, X: p.x, C: p.c}
        done = self.order[:stage]
        view = self.buf.at[tuple(slice(None) if a in done else here[a] for a in self.axes)]
        slot = stage + (p.dpn - 2 if Z in done else 0)
        return [
            remote(view, view, self.send.at[slot + k], self.recv.at[slot + k], device)
            for k, device in enumerate(p.partners(self.order[stage]))
        ]

    def advance(self):
        if self.at:
            for copy in self.copies(self.at - 1):
                copy.wait_recv()
        if self.at < len(self.order):
            for copy in self.copies(self.at):
                copy.start()
        self.at += 1

    def finish(self):
        while self.at <= len(self.order):
            self.advance()

    def drain(self):
        for stage in range(len(self.order)):
            for copy in self.copies(stage):
                copy.wait_send()


class Scatter:
    def __init__(self, place, acc, recvs, send, recv, order, sink):
        self.place, self.acc, self.recvs, self.send, self.recv = place, acc, recvs, send, recv
        self.order, self.sink = order, sink
        self.at = 0

    def view(self, stage, target):
        p = self.place
        here = {Z: p.dp, Y: p.y, X: p.x, C: p.c}
        here[self.order[stage]] = target
        known = self.order[: stage + 1]
        return tuple(here[a] if a in known else slice(None) for a in AXES)

    def copies(self, stage):
        p = self.place
        axis = self.order[stage]
        slot = stage + (p.dpn - 2 if Z in self.order[:stage] else 0)
        if axis == Z:
            targets = [(p.dp + k + 1) % p.dpn for k in range(p.dpn - 1)]
        else:
            targets = [1 - {Y: p.y, X: p.x, C: p.c}[axis]]
        return [
            remote(
                self.acc.at[self.view(stage, target)],
                self.recvs[stage].at[k],
                self.send.at[slot + k],
                self.recv.at[slot + k],
                device,
            )
            for k, (target, device) in enumerate(zip(targets, p.partners(axis)))
        ]

    def advance(self):
        last = len(self.order)
        if self.at:
            stage = self.at - 1
            copies = self.copies(stage)
            for copy in copies:
                copy.wait_recv()
            p = self.place
            where = self.view(stage, {Z: p.dp, Y: p.y, X: p.x, C: p.c}[self.order[stage]])
            if self.at < last and len(copies) == 1:
                self.acc[where] = self.acc[where] + self.recvs[stage][0]
            else:
                total = self.acc[where].astype(f32)
                for k in range(len(copies)):
                    total = total + self.recvs[stage][k].astype(f32)
                if self.at < last:
                    self.acc[where] = total.astype(bf16)
                else:
                    self.sink(total)
        if self.at < last:
            for copy in self.copies(self.at):
                copy.start()
        self.at += 1

    def finish(self):
        while self.at <= len(self.order):
            self.advance()

    def drain(self):
        for stage in range(len(self.order)):
            for copy in self.copies(stage):
                copy.wait_send()


class Shift:
    def __init__(self, copy):
        self.copy = copy
        self.at = 0

    def advance(self):
        if self.at:
            self.copy.wait_recv()
        else:
            self.copy.start()
        self.at += 1

    def finish(self):
        while self.at < 2:
            self.advance()

    def drain(self):
        self.copy.wait_send()


def heads_of(value):
    return value.reshape(HEADS, HD, value.shape[-1])


def per_head(value):
    return jnp.sum(heads_of(value), axis=1)


def spread(rows):
    return jnp.broadcast_to(rows[:, None, :], (HEADS, HD, rows.shape[-1])).reshape(D, rows.shape[-1])


def norm_scale(value):
    return lax.rsqrt(jnp.mean(value * value, axis=0, keepdims=True) + epsilon)


def norm_back(grad, normed, scale):
    return scale * (grad - normed * jnp.mean(grad * normed, axis=0, keepdims=True))


def one_head(pair, e):
    row = lax.broadcasted_iota(jnp.int32, pair.shape, 0)
    return jnp.where((row >= HD) == (e == 1), pair, jnp.zeros_like(pair))


def layer(dpn, *refs):
    (tok, pre, nbr, tab, gains, wq, wk, wv, wo, wi, wu, cot) = refs[:12]
    (out, ig, gq, gk, gv, go_, gi, gu, gg) = refs[12:21]
    (
        bufS, bufW, bufO, bufI, bufU, bufT, tokP, stage, xT, coT, niO, niP, qs, kvO, kvP, loc, near,
        nw, gate, lse, dlt, mid, bld, fi, y, gm, bias, G, hgR,
    ) = refs[21:50]
    recvs = [refs[50 + 4 * k : 54 + 4 * k] for k in range(len(SUMS))]
    ags, agr, rss, rsr, hs, hr, dms = refs[50 + 4 * len(SUMS) :]
    place = Place(dpn)
    dp, s = place.dp, place.s
    cy, cx, cc = place.y, place.x, place.c
    lead = (dpn, 2, 2, 2)
    nseq = 8
    nxt = (dp, (s + 1) % nseq)
    prv = (dp, (s + nseq - 1) % nseq)

    tok_in = [pltpu.make_async_copy(tok.at[b], stage.at[b], dms.at[b]) for b in range(NB)]
    for copy in tok_in:
        copy.start()
    for p in range(PAIRS):
        for i, w in enumerate((wq, wk, wv)):
            block = w[:, p * 128 : (p + 1) * 128]
            if p == 0:
                bufS[dp, cy, cx, cc, :, i * 128 : (i + 1) * 128] = block
            else:
                bufW[p - 1, dp, cy, cx, cc, :, i * 128 : (i + 1) * 128] = block
    bufS[dp, cy, cx, cc, :, 384:512] = gains[...]

    barrier = pltpu.get_barrier_semaphore()
    greet = [place.along(k + 1) for k in range(dpn - 1)]
    greet += [place.across(Y), place.across(X), place.across(C), nxt, prv]
    for device in greet:
        pl.semaphore_signal(barrier, inc=1, device_id=device, device_id_type=MESH)
    pl.semaphore_wait(barrier, len(greet))

    bufs = {W0: bufS, O: bufO}
    for k in range(3):
        bufs[W1 + k] = bufW.at[k]
    for k in range(2):
        bufs[T0 + k] = bufT.at[k]
        bufs[U0 + k] = bufU.at[k]
    for k in range(4):
        bufs[I0 + k] = bufI.at[k]
    comm = {}
    for k, (name, order) in enumerate(GATHERS):
        comm[name] = Gather(place, bufs[name], ags.at[k], agr.at[k], order)
    for b in range(NB):
        comm[H0 + b] = Shift(remote(tok.at[b], tokP.at[b], hs.at[b], hr.at[b], nxt))
        comm[B0 + b] = Shift(remote(tokP.at[b], hgR.at[b], hs.at[2 + b], hr.at[2 + b], prv))
    kept = []

    def sink(name):
        def put(total):
            if name < RU0:
                k = name - RI0
                gi[:, k * 512 : (k + 1) * 512] = total
            elif name < RO:
                k = name - RU0
                gu[:, k * 256 : (k + 1) * 256] = total
            elif name == RO:
                go_[...] = total[:, 0:512]
                kept.append(total[:, 513:514])
            else:
                at = slice((name - RQ0) * 128, (name - RQ0 + 1) * 128)
                for i, grad in enumerate((gq, gk, gv)):
                    grad[:, at] = total[:, i * 128 : (i + 1) * 128]

        return put

    accs = {RO: bufO}
    for k in range(2):
        accs[RU0 + k] = bufU.at[k]
    for k in range(4):
        accs[RI0 + k] = bufI.at[k]
        accs[RQ0 + k] = near.at[0, k, :, :, :, :, :, 0:384]
    for k, (name, order) in enumerate(SUMS):
        comm[name] = Scatter(place, accs[name], recvs[k], rss.at[k], rsr.at[k], order, sink(name))

    def tick(*label):
        for name in PLAN.get(label, ()):
            comm[name].advance()

    def need(label, *names):
        for name in BEFORE.get(label, ()):
            comm[name].advance()
        for name in names:
            comm[name].finish()

    bufO[dp, cy, cx, cc, :, 0:512] = wo[...]
    bufO[dp, cy, cx, cc, :, 512:640] = gains[...]
    for j in range(4):
        bufI[j, dp, cy, cx, cc] = wi[:, j * 512 : (j + 1) * 512]
    for q in range(2):
        bufU[q, dp, cy, cx, cc] = wu[:, q * 256 : (q + 1) * 256]
    for q in range(2):
        bufT[q, cy, cx, cc] = tab[:, q * 256 : (q + 1) * 256]
    tick(BEGIN)

    seg = s
    base = seg * SEG
    away = (seg == 0).astype(f32) * far

    def set_bias(b):
        q = lax.broadcasted_iota(jnp.int32, (1, SEG), 1)
        k = lax.broadcasted_iota(jnp.int32, (SEG, SEG), 0)
        limit = jnp.where(base + q < pre[b], jnp.maximum(q, pre[b] - 1 - base), q)
        bias[b] = jnp.where(k <= limit, 0.0, -far).astype(f32)

    cot_in = []
    for b in range(NB):
        tok_in[b].wait()
        xT[b] = stage[b].T
        cot_in.append(pltpu.make_async_copy(cot.at[b], stage.at[b], dms.at[b]))
        cot_in[b].start()
        tick(XT, b)
    set_bias(0)
    tick(BIAS, 0)
    for b in range(NB):
        cot_in[b].wait()
        coT[b] = stage[b].T
        tick(COT, b)
    set_bias(1)
    tick(BIAS, 1)
    need((NORM, 0), W0)

    again = bufS[..., 384:512].reshape(D, 128)[:, 0:1].astype(f32)

    def w3(p):
        return (bufS[..., 0:384] if p == 0 else bufW[p - 1]).reshape(D, 384)

    def own_norm(b):
        X = xT[b].astype(f32)
        niO[b] = (X * norm_scale(X) * again).astype(bf16)

    def own_proj(b, p):
        w = w3(p)
        kvO[b, p] = mm(niO[b], w[:, 128:384], 0, 0).astype(bf16)
        qs[b, p] = mm(w[:, 0:128], niO[b], 0, 0).astype(bf16) * jnp.asarray(0.125, bf16)

    def prev_norm(b):
        X = tokP[b].T.astype(f32)
        niP[b] = (X * norm_scale(X) * again).astype(bf16)

    def prev_proj(b, p):
        kvP[b, p] = mm(niP[b], w3(p)[:, 128:384], 0, 0).astype(bf16)

    def attend_own(b, p):
        ko, vo = kvO[b, p, :, 0:128], kvO[b, p, :, 128:256].T
        q2 = qs[b, p]
        for e in range(2):
            so = mm(ko, one_head(q2, e), 1, 0) + bias[b]
            top = jnp.max(so, axis=0, keepdims=True)
            eo = jnp.exp(so - top)
            rows = slice(e * HD, (e + 1) * HD)
            lse[b, 2 * p + e : 2 * p + e + 1, :] = top
            dlt[b, 2 * p + e : 2 * p + e + 1, :] = jnp.sum(eo, axis=0, keepdims=True)
            loc[b, p, rows] = mm(vo[rows], eo.astype(bf16), 1, 0)

    def attend_prev(b, p):
        kp, vp = kvP[b, p, :, 0:128], kvP[b, p, :, 128:256].T
        q2 = qs[b, p]
        for e in range(2):
            sp = mm(kp, one_head(q2, e), 1, 0)
            first = lse[b, 2 * p + e : 2 * p + e + 1, :]
            top = jnp.maximum(first, jnp.max(sp, axis=0, keepdims=True) - away)
            ep = jnp.exp(sp - (top + away))
            keep = jnp.exp(first - top)
            total = dlt[b, 2 * p + e : 2 * p + e + 1, :] * keep + jnp.sum(ep, axis=0, keepdims=True)
            rows = slice(e * HD, (e + 1) * HD)
            o = loc[b, p, rows] * keep + mm(vp[rows], ep.astype(bf16), 1, 0)
            loc[b, p, rows] = o / total
            lse[b, 2 * p + e : 2 * p + e + 1, :] = top + jnp.log(total)

    def remember(b):
        halves = [bufT[h].reshape(-1, 256) for h in range(2)]
        q = qs[b].reshape(D, SEG).astype(f32)
        row = lax.broadcasted_iota(jnp.int32, (halves[0].shape[0], SEG), 0)
        scores = []
        for k in range(KNN):
            hot = (row == nbr[b, k : k + 1, :]).astype(bf16)
            rows = jnp.concatenate([mm(half, hot, 0, 0) for half in halves], axis=0)
            near[b, k] = rows.astype(bf16).reshape(lead + (16, SEG))
            scores.append(per_head(q * rows))
        top = scores[0]
        for k in range(1, KNN):
            top = jnp.maximum(top, scores[k])
        scores = [jnp.exp(v - top) for v in scores]
        total = scores[0] + scores[1] + scores[2] + scores[3]
        for k in range(KNN):
            nw[b, k] = scores[k] / total

    def blend(b):
        cols = bufS[..., 384:512].reshape(D, 128).astype(f32)
        gvec, fgain = cols[:, 1:2], cols[:, 2:3]
        recalled = spread(nw[b, 0]) * near[b, 0].reshape(D, SEG).astype(f32)
        for k in range(1, KNN):
            recalled = recalled + spread(nw[b, k]) * near[b, k].reshape(D, SEG).astype(f32)
        local = loc[b].reshape(D, SEG)
        opened = jax.nn.sigmoid(per_head(local * gvec))
        gate[b] = opened
        wide = spread(opened)
        blended = (wide * recalled + (1.0 - wide) * local).astype(bf16)
        bld[b] = blended
        w = bufO[..., 0:512].reshape(D, D)
        middle = xT[b].astype(f32) + mm(w, blended, 0, 0)
        mid[b] = middle
        y[b] = middle
        fi[b] = (middle * norm_scale(middle) * fgain).astype(bf16)

    for b in range(NB):
        own_norm(b)
        tick(NORM, b)
    for p in range(PAIRS):
        for b in range(NB):
            need((PROJ, b, p), W0 + p)
            own_proj(b, p)
            tick(PROJ, b, p)
        for b in range(NB):
            attend_own(b, p)
            tick(OWN, b, p)

    def previous(b):
        need((PN, b), H0 + b)
        prev_norm(b)
        tick(PN, b)
        for p in range(PAIRS):
            prev_proj(b, p)
        tick(PP, b)
        for p in range(PAIRS):
            attend_prev(b, p)
            tick(PREV, b, p)

    for kind, b in FORWARD:
        if kind == PREV:
            previous(b)
        elif kind == REM:
            need((REM, b), T0, T1)
            remember(b)
            tick(REM, b)
        else:
            need((BLEND, b), O)
            blend(b)
            tick(BLEND, b)

    root = 0.7978845608028654
    def ffn(j, b):
        win = bufI[j].reshape(D, 512)
        wout = [bufU[q, j].reshape(512, 256) for q in range(2)]
        v = mm(win, fi[b], 0, 0)
        gh = mm(wout[0], coT[b, 0:256], 1, 0) + mm(wout[1], coT[b, 256:512], 1, 0)
        v2 = v * v
        t = jnp.tanh(root * v * (1.0 + 0.044715 * v2))
        half = 0.5 * (1.0 + t)
        hb = (v * half).astype(bf16)
        G[b, j, 0:512] = hb
        slope = half + 0.5 * v * (1.0 - t * t) * (root * (1.0 + 3 * 0.044715 * v2))
        gp = (gh * slope).astype(bf16)
        for q in range(2):
            at = slice(q * 256, (q + 1) * 256)
            y[b, at] = y[b, at] + mm(wout[q], hb, 0, 0)
        into = mm(win, gp, 1, 0)
        if j == 0:
            gm[b] = into
        else:
            gm[b] = gm[b] + into
        return gp

    for j in range(4):
        gps = []
        for b in range(NB):
            need((FFN, j, b), U0, U1, I0 + j)
            gps.append(ffn(j, b))
            tick(FFN, j, b)
        gin = mm(fi[0], gps[0], 1, 1) + mm(fi[1], gps[1], 1, 1)
        comm[I0 + j].drain()
        bufI[j] = gin.astype(bf16).reshape(lead + (16, 512))
        tick(GIN, j)
    for name, order in GATHERS:
        if not I0 <= name <= I3:
            comm[name].drain()
    for b in range(NB):
        comm[H0 + b].drain()
    for q in range(2):
        at = slice(q * 256, (q + 1) * 256)
        a = mm(G[0, :, 0:512].reshape(FF, SEG), coT[0, at], 1, 1)
        a = a + mm(G[1, :, 0:512].reshape(FF, SEG), coT[1, at], 1, 1)
        bufU[q] = a.astype(bf16).reshape(lead + (64, 256))
        tick(UG, q)

    out_copies = []
    cols = bufS[..., 384:512].reshape(D, 128).astype(f32)
    gvec, fgain = cols[:, 1:2], cols[:, 2:3]
    wout_a = bufO[..., 0:512].reshape(D, D)
    gwo = None
    ggv = None
    for b in range(NB):
        stage[b] = y[b].astype(bf16).T
        copy = pltpu.make_async_copy(stage.at[b], out.at[b], dms.at[b])
        copy.start()
        out_copies.append(copy)
        middle = mid[b]
        scale = norm_scale(middle)
        grad = coT[b].astype(f32) + norm_back(gm[b] * fgain, middle * scale, scale)
        gm[b] = grad
        gb = grad.astype(bf16)
        part = mm(bld[b], gb, 1, 1)
        gwo = part if gwo is None else gwo + part
        gbl = mm(wout_a, gb, 1, 0)
        local = loc[b].reshape(D, SEG)
        opened = gate[b]
        along = per_head(gbl * local)
        hits = [per_head(gbl * near[b, k].reshape(D, SEG).astype(f32)) for k in range(KNN)]
        mixed = hits[0] * nw[b, 0]
        for k in range(1, KNN):
            mixed = mixed + hits[k] * nw[b, k]
        ggate = (mixed - along) * opened * (1.0 - opened)
        wide = spread(ggate)
        part = jnp.sum(wide * local, axis=1, keepdims=True)
        ggv = part if ggv is None else ggv + part
        dlo = (spread(1.0 - opened) * gbl + wide * gvec).astype(bf16)
        fi[b] = dlo
        dots = per_head(dlo.astype(f32) * local)
        dlt[b] = dots
        dq = None
        for k in range(KNN):
            weight = spread(nw[b, k] * opened * (hits[k] - mixed) * 0.125)
            part = weight * near[b, k].reshape(D, SEG).astype(f32)
            dq = part if dq is None else dq + part
        y[b] = dq
        tick(CPRE, b)
    bufO[..., 0:512] = gwo.astype(bf16).reshape(lead + (16, 512))
    bufO[..., 512:640] = jnp.broadcast_to(ggv, (D, 128)).astype(bf16).reshape(lead + (16, 128))
    tick(GWO)

    def retreat(b, p, kv, own):
        k2, v2 = kv[b, p, :, 0:128], kv[b, p, :, 128:256]
        kt = k2.T
        q2 = qs[b, p]
        d2 = fi[b, pl.ds(p * 128, 128), :]
        for e in range(2):
            rows = slice(e * HD, (e + 1) * HD)
            sc = mm(k2, one_head(q2, e), 1, 0)
            if own:
                pr = jnp.exp((sc + bias[b]) - lse[b, 2 * p + e : 2 * p + e + 1, :])
            else:
                pr = jnp.exp(sc - (lse[b, 2 * p + e : 2 * p + e + 1, :] + away))
            dpr = mm(v2, one_head(d2, e), 1, 0)
            ds = (pr * (dpr - dlt[b, 2 * p + e : 2 * p + e + 1, :])).astype(bf16)
            dv = mm(d2[rows], pr.astype(bf16), 1, 1).astype(bf16)
            dk = mm(q2[rows], ds, 1, 1).astype(bf16)
            dq = mm(kt[rows], ds, 1, 0) * 0.125
            at = pl.ds(p * 128 + e * HD, HD)
            low, high = e * HD, (e + 1) * HD
            if own:
                G[b, p, low:high] = (y[b, at, :] + dq).astype(bf16)
                G[b, p, 128 + low : 128 + high] = dk
                G[b, p, 256 + low : 256 + high] = dv
            else:
                y[b, at, :] = y[b, at, :] + dq
                G[b, p, 384 + low : 384 + high] = dk
                G[b, p, 512 + low : 512 + high] = dv

    def send_back(b):
        sent = mm(w3(0)[:, 128:384], G[b, 0, 384:640], 1, 0)
        for p in range(1, PAIRS):
            sent = sent + mm(w3(p)[:, 128:384], G[b, p, 384:640], 1, 0)
        tokP[b] = sent.astype(bf16)

    for b in range(NB):
        for p in range(PAIRS):
            retreat(b, p, kvP, False)
            tick(RP, b, p)
        send_back(b)
        tick(SEND, b)
    for p in range(PAIRS):
        for b in range(NB):
            retreat(b, p, kvO, True)
            tick(ROW, b, p)
        quer = mm(niO[0], G[0, p, 0:128], 1, 1) + mm(niO[1], G[1, p, 0:128], 1, 1)
        near[0, p, ..., 0:128] = quer.astype(bf16).reshape(lead + (16, 128))
        rest = mm(niO[0], G[0, p, 128:384], 1, 1)
        rest = rest + mm(niP[0], G[0, p, 384:640], 1, 1)
        rest = rest + mm(niO[1], G[1, p, 128:384], 1, 1)
        rest = rest + mm(niP[1], G[1, p, 384:640], 1, 1)
        near[0, p, ..., 128:384] = rest.astype(bf16).reshape(lead + (16, 256))
        tick(DW, p)

    def finish(b):
        total = mm(w3(0), G[b, 0, 0:384], 1, 0)
        for p in range(1, PAIRS):
            total = total + mm(w3(p), G[b, p, 0:384], 1, 0)
        total = total + hgR[b].astype(f32)
        X = xT[b].astype(f32)
        scale = norm_scale(X)
        res = gm[b] + norm_back(total * again, X * scale, scale)
        mid[b] = res.T
        copy = pltpu.make_async_copy(mid.at[b], ig.at[b], dms.at[2 + b])
        copy.start()
        return copy

    ends = []
    for b in range(NB):
        need((FIN, b), B0 + b)
        ends.append(finish(b))
        tick(FIN, b)
    need((END,), *(name for name, order in SUMS))
    own = gains[...].astype(f32)
    fsum = jnp.sum(gi[...] * wi[...].astype(f32), axis=1, keepdims=True) / own[:, 2:3]
    asum = gq[...] * wq[...].astype(f32) + gk[...] * wk[...].astype(f32) + gv[...] * wv[...].astype(f32)
    asum = jnp.sum(asum, axis=1, keepdims=True) / own[:, 0:1]
    lane = lax.broadcasted_iota(jnp.int32, (16, 128), 1)
    here = lax.broadcasted_iota(jnp.int32, (16, 128), 0) == lane
    for i, col in enumerate((asum, kept[0], fsum)):
        gg[i : i + 1, :] = jnp.sum(jnp.where(here, col, 0.0), axis=0, keepdims=True)
    for name, order in SUMS:
        comm[name].drain()
    for b in range(NB):
        comm[B0 + b].drain()
    for copy in out_copies + ends:
        copy.wait()


def fused(dpn, tokens, prefix, neighbours, table, attn_gain, w_query, w_key, w_value, gate_vector,
          w_output, ffn_gain, w_inner, w_outer, cotangent):
    gains = jnp.pad(jnp.stack([attn_gain, gate_vector, ffn_gain], axis=1), ((0, 0), (0, 125)))
    vm = pl.BlockSpec(memory_space=pltpu.VMEM)
    hb = pl.BlockSpec(memory_space=pl.ANY)
    sm = pl.BlockSpec(memory_space=pltpu.SMEM)
    V = pltpu.VMEM
    lead = (dpn, 2, 2, 2)
    sq = (NB, D, SEG)

    sizes = {Z: dpn, Y: 2, X: 2, C: 2}

    def landing(name, order):
        if name < RU0:
            block = (16, 512)
        elif name < RO:
            block = (64, 256)
        else:
            block = (16, 640) if name == RO else (16, 384)
        shapes = []
        for stage, axis in enumerate(order):
            left = tuple(sizes[a] for a in AXES if a not in order[: stage + 1])
            shapes.append(V((sizes[axis] - 1,) + left + block, bf16))
        return shapes

    scratch = [
        V(lead + (16, 512), bf16),
        V((PAIRS - 1,) + lead + (16, 384), bf16),
        V(lead + (16, 640), bf16),
        V((4,) + lead + (16, 512), bf16),
        V((2,) + lead + (64, 256), bf16),
        V((2, 2, 2, 2, table.shape[0], 256), bf16),
        V(sq, bf16),
        V(sq, bf16),
        V(sq, bf16),
        V(sq, bf16),
        V(sq, bf16),
        V(sq, bf16),
        V((NB, PAIRS, 128, SEG), bf16),
        V((NB, PAIRS, SEG, 256), bf16),
        V((NB, PAIRS, SEG, 256), bf16),
        V((NB, PAIRS, 128, SEG), f32),
        V((NB, KNN) + lead + (16, SEG), bf16),
        V((NB, KNN, HEADS, SEG), f32),
        V((NB, HEADS, SEG), f32),
        V((NB, HEADS, SEG), f32),
        V((NB, HEADS, SEG), f32),
        V(sq, f32),
        V(sq, bf16),
        V(sq, bf16),
        V(sq, f32),
        V(sq, f32),
        V((NB, SEG, SEG), f32),
        V((NB, PAIRS, 640, SEG), bf16),
        V(sq, bf16),
    ]
    for name, order in SUMS:
        scratch += landing(name, order)
    dma = pltpu.SemaphoreType.DMA
    scratch += [
        dma((len(GATHERS), dpn + 2)), dma((len(GATHERS), dpn + 2)), dma((len(SUMS), dpn + 2)),
        dma((len(SUMS), dpn + 2)), dma((4,)), dma((4,)), dma((4,)),
    ]
    rows = w_query.shape[0]
    sds = jax.ShapeDtypeStruct
    out = pl.pallas_call(
        lambda *refs: layer(dpn, *refs),
        name="layer",
        out_shape=(
            sds(tokens.shape, bf16),
            sds(tokens.shape, f32),
            sds((rows, D), f32),
            sds((rows, D), f32),
            sds((rows, D), f32),
            sds((rows, D), f32),
            sds((rows, FF), f32),
            sds(w_outer.shape, f32),
            sds((8, 128), f32),
        ),
        in_specs=[hb, sm, vm, vm, vm, vm, vm, vm, vm, vm, vm, hb],
        out_specs=(hb, hb) + (vm,) * 7,
        scratch_shapes=scratch,
        compiler_params=pltpu.CompilerParams(
            collective_id=0, has_side_effects=True, vmem_limit_bytes=63 * 2**20
        ),
    )(
        tokens, prefix, neighbours.transpose(0, 2, 1), table, gains, w_query, w_key, w_value, w_output,
        w_inner, w_outer, cotangent,
    )
    return settle(out)


def settle_kernel(*refs):
    big, gg = refs[:8], refs[8]
    to, vectors = refs[9:17], refs[17:20]
    bufs, sems, outs = refs[20:28], refs[28], refs[29]
    pieces = []
    for src, buf, dst in zip(big, bufs, to):
        if len(src.shape) == 3:
            for i in range(2):
                for j in range(2):
                    at = (i, pl.ds(j * 256, 256))
                    pieces.append((src.at[at], buf.at[at], dst.at[at]))
        else:
            pieces.append((src, buf, dst))
    come = [pltpu.make_async_copy(a, b, sems.at[k]) for k, (a, b, c) in enumerate(pieces)]
    leave = [pltpu.make_async_copy(b, c, outs.at[k]) for k, (a, b, c) in enumerate(pieces)]
    for copy in come:
        copy.start()
    for i, vector in enumerate(vectors):
        vector[...] = gg[i, 0:16]
    for first, then in zip(come, leave):
        first.wait()
        then.start()
    for copy in leave:
        copy.wait()


def settle(out):
    hb = pl.BlockSpec(memory_space=pl.ANY)
    vm = pl.BlockSpec(memory_space=pltpu.VMEM)
    sds = jax.ShapeDtypeStruct
    res = pl.pallas_call(
        settle_kernel,
        name="settle",
        out_shape=tuple(sds(v.shape, v.dtype) for v in out[:8]) + (sds((16,), f32),) * 3,
        in_specs=[hb] * 8 + [vm],
        out_specs=(hb,) * 8 + (vm,) * 3,
        scratch_shapes=[pltpu.VMEM(v.shape, v.dtype) for v in out[:8]]
        + [pltpu.SemaphoreType.DMA((14,)), pltpu.SemaphoreType.DMA((14,))],
    )(*out)
    return (
        res[0], res[1], res[8], res[2], res[3], res[4], res[9], res[5], res[10], res[6], res[7],
    )


masked_floor = -1000000000.0


def from_behind(value, axis, by):
    count = lax.axis_size(axis)
    pairs = [(i, i + by) for i in range(count) if 0 <= i + by < count]
    return lax.ppermute(value, axis, pairs)


def times_plain(left, right):
    return jnp.dot(left, right, preferred_element_type=jnp.float32)


def times_first_t(left, right):
    return lax.dot_general(
        left, right, (((0,), (0,)), ((), ())), preferred_element_type=jnp.float32
    )


def times_second_t(left, right):
    return lax.dot_general(
        left, right, (((1,), (1,)), ((), ())), preferred_element_type=jnp.float32
    )


def gelu_tanh(values):
    return jax.nn.gelu(values, approximate=True)


def rms_scale(values):
    return lax.rsqrt(jnp.mean(values * values, axis=-1, keepdims=True) + epsilon)


def norm_back_rows(grad_normed, normed, scale):
    return scale * (grad_normed - normed * jnp.mean(grad_normed * normed, axis=-1, keepdims=True))


def split_heads(rows):
    return rows.reshape(rows.shape[0], HEADS, HD).transpose(1, 0, 2)


def merge_heads(stacked):
    return stacked.transpose(1, 0, 2).reshape(stacked.shape[1], D)


def visible_mask(segment, prefix_len):
    query_pos = segment * SEG + lax.iota(jnp.int32, SEG)
    key_pos = (segment - 1) * SEG + lax.iota(jnp.int32, 2 * SEG)
    return (key_pos[None, :] >= 0) & (
        (key_pos[None, :] <= query_pos[:, None])
        | (query_pos[:, None] < prefix_len) & (key_pos[None, :] < prefix_len)
    )


def fetch_attention(attn_gain, w_query, w_key, w_value, gate_vector, w_output):
    return (
        lax.all_gather(attn_gain, ("dp", "seq"), axis=0, tiled=True),
        lax.all_gather(w_query, ("dp", "seq"), axis=0, tiled=True),
        lax.all_gather(w_key, ("dp", "seq"), axis=0, tiled=True),
        lax.all_gather(w_value, ("dp", "seq"), axis=0, tiled=True),
        lax.all_gather(gate_vector, ("dp", "seq"), axis=0, tiled=True),
        lax.all_gather(w_output, ("dp", "seq"), axis=0, tiled=True),
    )


def fetch_feedforward(ffn_gain, w_inner, w_outer):
    return (
        lax.all_gather(ffn_gain, ("dp", "seq"), axis=0, tiled=True),
        lax.all_gather(w_inner, ("dp", "seq"), axis=0, tiled=True),
        lax.all_gather(w_outer, ("dp", "seq"), axis=0, tiled=True),
    )


def forward_pass(tokens_row, visible, near_b, attn_set, ffn_set):
    attn_gain, w_query, w_key, w_value, gate_vector, w_output = attn_set
    ffn_gain, w_inner, w_outer = ffn_set
    rows_count = tokens_row.shape[0]
    inputs_f = tokens_row.astype(jnp.float32)
    scale_one = rms_scale(inputs_f)
    normed_one = inputs_f * scale_one
    normed_in = (normed_one * attn_gain.astype(jnp.float32)).astype(jnp.bfloat16)
    query_b = times_plain(normed_in, w_query).astype(jnp.bfloat16)
    key_b = times_plain(normed_in, w_key).astype(jnp.bfloat16)
    value_b = times_plain(normed_in, w_value).astype(jnp.bfloat16)
    key_prev, value_prev = from_behind((key_b, value_b), "seq", 1)
    key_all = jnp.concatenate([key_prev, key_b], axis=0)
    value_all = jnp.concatenate([value_prev, value_b], axis=0)
    visible_f = visible.astype(jnp.float32)

    def head_forward(operands):
        query_h, key_h, value_h = operands
        scores = jnp.where(visible, times_second_t(query_h, key_h) * 0.125, masked_floor)
        row_max = jnp.max(scores, axis=1, keepdims=True)
        exponent = jnp.exp(scores - row_max) * visible_f
        row_sum = jnp.sum(exponent, axis=1, keepdims=True)
        attn_probs = (exponent / row_sum).astype(jnp.bfloat16)
        return (times_plain(attn_probs, value_h), (row_max + jnp.log(row_sum))[:, 0])

    local_h, log_norm = lax.map(
        head_forward, (split_heads(query_b), split_heads(key_all), split_heads(value_all))
    )
    local_t = local_h.transpose(1, 0, 2)
    query_t = query_b.reshape(rows_count, HEADS, HD)
    near_scores = (
        jnp.einsum("shd,skhd->shk", query_t, near_b, preferred_element_type=jnp.float32) * 0.125
    )
    near_exp = jnp.exp(near_scores - jnp.max(near_scores, axis=-1, keepdims=True))
    near_weights = near_exp / jnp.sum(near_exp, axis=-1, keepdims=True)
    recalled = jnp.einsum("shk,skhd->shd", near_weights, near_b, preferred_element_type=jnp.float32)
    gate_h = gate_vector.astype(jnp.float32).reshape(HEADS, HD)
    gate_open = jax.nn.sigmoid(jnp.sum(local_t * gate_h, axis=-1, keepdims=True))
    blended_b = (
        (gate_open * recalled + (1.0 - gate_open) * local_t)
        .reshape(rows_count, D)
        .astype(jnp.bfloat16)
    )
    middle = inputs_f + times_plain(blended_b, w_output)
    scale_two = rms_scale(middle)
    normed_two = middle * scale_two
    ffn_in = (normed_two * ffn_gain.astype(jnp.float32)).astype(jnp.bfloat16)
    hidden_pre = times_plain(ffn_in, w_inner)
    hidden_b = gelu_tanh(hidden_pre).astype(jnp.bfloat16)
    result = (middle + times_plain(hidden_b, w_outer)).astype(jnp.bfloat16)
    kept = (
        scale_one,
        normed_one,
        normed_in,
        query_b,
        key_all,
        value_all,
        log_norm,
        local_t,
        near_weights,
        recalled,
        gate_open,
        blended_b,
        scale_two,
        normed_two,
        ffn_in,
        hidden_pre,
        hidden_b,
    )
    return (result, kept)


def backward_pass(kept, cot_row, visible, near_b, attn_set, ffn_set):
    (
        scale_one,
        normed_one,
        normed_in,
        query_b,
        key_all,
        value_all,
        log_norm,
        local_t,
        near_weights,
        recalled,
        gate_open,
        blended_b,
        scale_two,
        normed_two,
        ffn_in,
        hidden_pre,
        hidden_b,
    ) = kept
    attn_gain, w_query, w_key, w_value, gate_vector, w_output = attn_set
    ffn_gain, w_inner, w_outer = ffn_set
    rows_count = cot_row.shape[0]
    dout = cot_row.astype(jnp.float32)
    grad_outer = times_first_t(hidden_b, cot_row)
    grad_hidden = times_second_t(cot_row, w_outer)
    unused_value, gelu_pull = jax.vjp(gelu_tanh, hidden_pre)
    grad_pre = gelu_pull(grad_hidden)[0].astype(jnp.bfloat16)
    grad_inner = times_first_t(ffn_in, grad_pre)
    grad_ffn_in = times_second_t(grad_pre, w_inner)
    grad_ffn_gain = jnp.sum(grad_ffn_in * normed_two, axis=0)
    grad_middle = dout + norm_back_rows(
        grad_ffn_in * ffn_gain.astype(jnp.float32), normed_two, scale_two
    )
    grad_branch_b = grad_middle.astype(jnp.bfloat16)
    grad_output = times_first_t(blended_b, grad_branch_b)
    grad_blended = times_second_t(grad_branch_b, w_output).reshape(rows_count, HEADS, HD)
    gate_h = gate_vector.astype(jnp.float32).reshape(HEADS, HD)
    grad_recalled = gate_open * grad_blended
    grad_gate = (
        jnp.sum(grad_blended * (recalled - local_t), axis=-1, keepdims=True)
        * gate_open
        * (1.0 - gate_open)
    )
    grad_gate_vector = jnp.sum(grad_gate * local_t, axis=0).reshape(D)
    grad_local_b = (
        ((1.0 - gate_open) * grad_blended + grad_gate * gate_h)
        .astype(jnp.bfloat16)
        .transpose(1, 0, 2)
    )
    grad_near_w = jnp.einsum(
        "shd,skhd->shk", grad_recalled, near_b, preferred_element_type=jnp.float32
    )
    grad_near = near_weights * (
        grad_near_w - jnp.sum(near_weights * grad_near_w, axis=-1, keepdims=True)
    )
    grad_query_near = (
        jnp.einsum("shk,skhd->shd", grad_near, near_b, preferred_element_type=jnp.float32) * 0.125
    )
    visible_f = visible.astype(jnp.float32)

    def head_backward(operands):
        query_h, key_h, value_h, grad_h, norm_h = operands
        scores = jnp.where(visible, times_second_t(query_h, key_h) * 0.125, masked_floor)
        attn_probs = jnp.exp(scores - norm_h[:, None]) * visible_f
        grad_probs = times_second_t(grad_h, value_h)
        grad_scores = (
            attn_probs * (grad_probs - jnp.sum(attn_probs * grad_probs, axis=1, keepdims=True))
        ).astype(jnp.bfloat16)
        return (
            times_plain(grad_scores, key_h) * 0.125,
            times_first_t(grad_scores, query_h) * 0.125,
            times_first_t(attn_probs.astype(jnp.bfloat16), grad_h),
        )

    grad_query_h, grad_key_h, grad_value_h = lax.map(
        head_backward,
        (
            split_heads(query_b),
            split_heads(key_all),
            split_heads(value_all),
            grad_local_b,
            log_norm,
        ),
    )
    grad_key_all = merge_heads(grad_key_h)
    grad_value_all = merge_heads(grad_value_h)
    later_key, later_value = (
        from_behind(grad_key_all[:rows_count].astype(jnp.bfloat16), "seq", -1).astype(jnp.float32),
        from_behind(grad_value_all[:rows_count].astype(jnp.bfloat16), "seq", -1).astype(
            jnp.float32
        ),
    )
    grad_query_b = (merge_heads(grad_query_h) + grad_query_near.reshape(rows_count, D)).astype(
        jnp.bfloat16
    )
    grad_key_b = (grad_key_all[rows_count:] + later_key).astype(jnp.bfloat16)
    grad_value_b = (grad_value_all[rows_count:] + later_value).astype(jnp.bfloat16)
    grad_query = times_first_t(normed_in, grad_query_b)
    grad_key = times_first_t(normed_in, grad_key_b)
    grad_value = times_first_t(normed_in, grad_value_b)
    grad_normed_in = (
        times_second_t(grad_query_b, w_query)
        + times_second_t(grad_key_b, w_key)
        + times_second_t(grad_value_b, w_value)
    )
    grad_attn_gain = jnp.sum(grad_normed_in * normed_one, axis=0)
    input_grad = grad_middle + norm_back_rows(
        grad_normed_in * attn_gain.astype(jnp.float32), normed_one, scale_one
    )
    grads = (
        grad_attn_gain,
        grad_query,
        grad_key,
        grad_value,
        grad_gate_vector,
        grad_output,
        grad_ffn_gain,
        grad_inner,
        grad_outer,
    )
    return (grads, input_grad)


def plain(
    tokens,
    prefix,
    neighbours,
    table,
    attn_gain,
    w_query,
    w_key,
    w_value,
    gate_vector,
    w_output,
    ffn_gain,
    w_inner,
    w_outer,
    cotangent,
):
    full_table = lax.all_gather(table, "seq", axis=0, tiled=True)
    segment = lax.axis_index("seq")
    rows_count = tokens.shape[1]
    outputs = []
    input_grads = []
    running = ()
    for micro_batch in range(tokens.shape[0]):
        visible = visible_mask(segment, prefix[micro_batch])
        near_b = jnp.take(full_table, neighbours[micro_batch].reshape(-1), axis=0).reshape(
            rows_count, KNN, HEADS, HD
        )
        attn_fwd = fetch_attention(attn_gain, w_query, w_key, w_value, gate_vector, w_output)
        ffn_fwd = fetch_feedforward(ffn_gain, w_inner, w_outer)
        result, kept = forward_pass(tokens[micro_batch], visible, near_b, attn_fwd, ffn_fwd)
        attn_back = fetch_attention(attn_gain, w_query, w_key, w_value, gate_vector, w_output)
        ffn_back = fetch_feedforward(ffn_gain, w_inner, w_outer)
        grads, input_grad = backward_pass(
            kept, cotangent[micro_batch], visible, near_b, attn_back, ffn_back
        )
        if micro_batch == 0:
            running = grads
        else:
            running = tuple((earlier + increment for earlier, increment in zip(running, grads)))
        outputs.append(result)
        input_grads.append(input_grad)
    shares = lax.psum_scatter(running, ("dp", "seq"), scatter_dimension=0, tiled=True)
    return (
        jnp.stack(outputs),
        jnp.stack(input_grads),
        shares[0],
        shares[1],
        shares[2],
        shares[3],
        shares[4],
        shares[5],
        shares[6],
        shares[7],
        shares[8],
    )


def solution(mesh):
    dpn = mesh.shape["dp"]

    def local(*args):
        if mesh.shape["seq"] == 8 and args[5].shape[0] == 16:
            return fused(dpn, *args)
        return plain(*args)

    rows = P(("dp", "seq"))
    wide = P(("dp", "seq"), None)
    block = P("dp", "seq", None)
    return jax.shard_map(
        local,
        mesh=mesh,
        in_specs=(
            block, P("dp"), block, P("seq", None), rows, wide, wide, wide, rows, wide, rows, wide, wide, block,
        ),
        out_specs=(block, block, rows, wide, wide, wide, rows, wide, rows, wide, wide),
        check_vma=False,
    )
```

```python
import jax
import jax.numpy as jnp
from jax import lax
from jax.experimental import pallas as pl
from jax.experimental.pallas import tpu as pltpu
from jax.sharding import PartitionSpec as P

D = 512
HEADS = 8
HD = 64
KNN = 4
SEG = 512
FF = 2048
PAIRS = 4
NB = 2
MESH = pl.DeviceIdType.MESH

epsilon = 1e-06
far = 1e30
f32 = jnp.float32
bf16 = jnp.bfloat16


def mm(left, right, over_left, over_right):
    return lax.dot_general(
        left, right, (((over_left,), (over_right,)), ((), ())), preferred_element_type=f32
    )


(W0, W1, W2, W3, T0, T1, O, U0, U1, I0, I1, I2, I3,
 H0, H1, B0, B1, RI0, RI1, RI2, RI3, RU0, RU1, RO, RQ0, RQ1, RQ2, RQ3) = range(28)
(BEGIN, XT, BIAS, COT, NORM, PROJ, OWN, PN, PP, PREV, REM, BLEND, FFN, GIN, UG, CPRE, GWO, RP, SEND, ROW, DW, FIN, END) = range(23)
Z, Y, X, C = range(4)

GATHERS = (
    (W0, (Z, X, Y, C)),
    (W1, (Z, X, Y, C)),
    (W2, (Y, Z, X, C)),
    (W3, (Y, Z, X, C)),
    (T0, (X, Y, C)),
    (T1, (Y, X, C)),
    (O, (Y, Z, X, C)),
    (U0, (Z, X, Y, C)),
    (U1, (Z, Y, X, C)),
    (I0, (Y, Z, X, C)),
    (I1, (Z, Y, X, C)),
    (I2, (Z, X, Y, C)),
    (I3, (Z, X, Y, C)),
)
SUMS = (
    (RI0, (C, Y, X, Z)),
    (RI1, (C, Y, X, Z)),
    (RI2, (C, Y, Z, X)),
    (RI3, (C, Y, X, Z)),
    (RU0, (C, X, Z, Y)),
    (RU1, (C, Y, Z, X)),
    (RO, (C, X, Z, Y)),
    (RQ0, (C, Y, X, Z)),
    (RQ1, (C, X, Y, Z)),
    (RQ2, (C, Y, Z, X)),
    (RQ3, (C, X, Y, Z)),
)
FORWARD = ((REM, 0), (REM, 1), (PREV, 0), (PREV, 1), (BLEND, 0), (BLEND, 1))
PLAN = {
    (BEGIN,): (W0, H0, T0),
    (XT, 0): (W2,),
    (COT, 1): (O, I0, W1, W3, T1),
    (OWN, 1, 0): (U0, W1, W3, T1),
    (PROJ, 1, 2): (U1, I1, W3, I0),
    (OWN, 1, 2): (H1, I3, O, U0, I0),
    (REM, 0): (I2, O, U1, I1, I3),
    (PN, 0): (U0, I2),
    (PREV, 0, 0): (I1, I3, U1),
    (PREV, 0, 2): (I2,),
    (PREV, 1, 2): (I1, I3),
    (PREV, 1, 3): (U0, U1, I2, I1, I3),
    (CPRE, 1): (RI0, RI1, RI2, RI3, RU0, RU1),
    (RP, 0, 3): (RO, RI0, RI1, RI2, RI3, RU0, RU1),
    (SEND, 0): (B0, RO),
    (DW, 1): (B1, RQ0, RQ1, RI0, RU0, RO, RI1, RI2, RI3, RQ0, RQ1),
    (DW, 3): (RQ2, RQ3, RI0, RI1, RI3, RU1, RO, RQ0, RQ1, RQ2, RQ3, RI2, RU0),
    (FIN, 0): (RI0, RI2, RO, RQ0, RQ1, RI1, RI3, RU0, RQ2, RQ3),
}
BEFORE = {
    (NORM, 0): (W2, W0, T0, W3, W1, I0, O, W2, W0, T1, W1, T0, W3, T0, W2, W0, I0, O, T1, W2, W1, W0),
    (PN, 0): (H0,),
    (PN, 1): (H1,),
    (FFN, 0, 0): (I2, U0, U1),
    (FIN, 0): (B0,),
    (FIN, 1): (B1,),
    (END,): (RU1, RQ0, RQ3, RQ1, RQ2, RU1, RQ2, RQ3),
}


class Place:
    def __init__(self, dpn):
        self.dpn = dpn
        self.dp = lax.axis_index("dp")
        self.s = lax.axis_index("seq")
        self.c = self.s % 2
        self.x = (self.s // 2) % 2
        self.y = self.s // 4

    def across(self, axis):
        if axis == C:
            return (self.dp, self.s + 1 - 2 * self.c)
        if axis == X:
            return (self.dp, self.s + 2 * (1 - 2 * self.x))
        return (self.dp, self.s + 4 * (1 - 2 * self.y))

    def along(self, step):
        return ((self.dp + step) % self.dpn, self.s)

    def partners(self, axis):
        if axis == Z:
            return [self.along(k + 1) for k in range(self.dpn - 1)]
        return [self.across(axis)]


def remote(src, dst, send, recv, device):
    return pltpu.make_async_remote_copy(
        src_ref=src, dst_ref=dst, send_sem=send, recv_sem=recv, device_id=device, device_id_type=MESH
    )


AXES = (Z, Y, X, C)


class Gather:
    def __init__(self, place, buf, send, recv, order):
        self.place, self.buf, self.send, self.recv, self.order = place, buf, send, recv, order
        self.axes = AXES if Z in order else AXES[1:]
        self.at = 0

    def copies(self, stage):
        p = self.place
        here = {Z: p.dp, Y: p.y, X: p.x, C: p.c}
        done = self.order[:stage]
        view = self.buf.at[tuple(slice(None) if a in done else here[a] for a in self.axes)]
        slot = stage + (p.dpn - 2 if Z in done else 0)
        return [
            remote(view, view, self.send.at[slot + k], self.recv.at[slot + k], device)
            for k, device in enumerate(p.partners(self.order[stage]))
        ]

    def advance(self):
        if self.at:
            for copy in self.copies(self.at - 1):
                copy.wait_recv()
        if self.at < len(self.order):
            for copy in self.copies(self.at):
                copy.start()
        self.at += 1

    def finish(self):
        while self.at <= len(self.order):
            self.advance()

    def drain(self):
        for stage in range(len(self.order)):
            for copy in self.copies(stage):
                copy.wait_send()


class Scatter:
    def __init__(self, place, acc, recvs, send, recv, order, sink):
        self.place, self.acc, self.recvs, self.send, self.recv = place, acc, recvs, send, recv
        self.order, self.sink = order, sink
        self.at = 0

    def view(self, stage, target):
        p = self.place
        here = {Z: p.dp, Y: p.y, X: p.x, C: p.c}
        here[self.order[stage]] = target
        known = self.order[: stage + 1]
        return tuple(here[a] if a in known else slice(None) for a in AXES)

    def copies(self, stage):
        p = self.place
        axis = self.order[stage]
        slot = stage + (p.dpn - 2 if Z in self.order[:stage] else 0)
        if axis == Z:
            targets = [(p.dp + k + 1) % p.dpn for k in range(p.dpn - 1)]
        else:
            targets = [1 - {Y: p.y, X: p.x, C: p.c}[axis]]
        return [
            remote(
                self.acc.at[self.view(stage, target)],
                self.recvs[stage].at[k],
                self.send.at[slot + k],
                self.recv.at[slot + k],
                device,
            )
            for k, (target, device) in enumerate(zip(targets, p.partners(axis)))
        ]

    def advance(self):
        last = len(self.order)
        if self.at:
            stage = self.at - 1
            copies = self.copies(stage)
            for copy in copies:
                copy.wait_recv()
            p = self.place
            where = self.view(stage, {Z: p.dp, Y: p.y, X: p.x, C: p.c}[self.order[stage]])
            if self.at < last and len(copies) == 1:
                self.acc[where] = self.acc[where] + self.recvs[stage][0]
            else:
                total = self.acc[where].astype(f32)
                for k in range(len(copies)):
                    total = total + self.recvs[stage][k].astype(f32)
                if self.at < last:
                    self.acc[where] = total.astype(bf16)
                else:
                    self.sink(total)
        if self.at < last:
            for copy in self.copies(self.at):
                copy.start()
        self.at += 1

    def finish(self):
        while self.at <= len(self.order):
            self.advance()

    def drain(self):
        for stage in range(len(self.order)):
            for copy in self.copies(stage):
                copy.wait_send()


class Shift:
    def __init__(self, copy):
        self.copy = copy
        self.at = 0

    def advance(self):
        if self.at:
            self.copy.wait_recv()
        else:
            self.copy.start()
        self.at += 1

    def finish(self):
        while self.at < 2:
            self.advance()

    def drain(self):
        self.copy.wait_send()


def heads_of(value):
    return value.reshape(HEADS, HD, value.shape[-1])


def per_head(value):
    return jnp.sum(heads_of(value), axis=1)


def spread(rows):
    return jnp.broadcast_to(rows[:, None, :], (HEADS, HD, rows.shape[-1])).reshape(D, rows.shape[-1])


def norm_scale(value):
    return lax.rsqrt(jnp.mean(value * value, axis=0, keepdims=True) + epsilon)


def norm_back(grad, normed, scale):
    return scale * (grad - normed * jnp.mean(grad * normed, axis=0, keepdims=True))


def one_head(pair, e):
    row = lax.broadcasted_iota(jnp.int32, pair.shape, 0)
    return jnp.where((row >= HD) == (e == 1), pair, jnp.zeros_like(pair))


def layer(dpn, *refs):
    (tok, pre, nbr, tab, gains, wq, wk, wv, wo, wi, wu, cot) = refs[:12]
    (out, ig, gq, gk, gv, go_, gi, gu, gg) = refs[12:21]
    (
        bufS, bufW, bufO, bufI, bufU, bufT, tokP, stage, xT, coT, niO, niP, qs, kvO, kvP, loc, near,
        nw, gate, lse, dlt, mid, bld, fi, y, gm, bias, G, hgR,
    ) = refs[21:50]
    recvs = [refs[50 + 4 * k : 54 + 4 * k] for k in range(len(SUMS))]
    ags, agr, rss, rsr, hs, hr, dms = refs[50 + 4 * len(SUMS) :]
    place = Place(dpn)
    dp, s = place.dp, place.s
    cy, cx, cc = place.y, place.x, place.c
    lead = (dpn, 2, 2, 2)
    nseq = 8
    nxt = (dp, (s + 1) % nseq)
    prv = (dp, (s + nseq - 1) % nseq)

    tok_in = [pltpu.make_async_copy(tok.at[b], stage.at[b], dms.at[b]) for b in range(NB)]
    for copy in tok_in:
        copy.start()
    for p in range(PAIRS):
        for i, w in enumerate((wq, wk, wv)):
            block = w[:, p * 128 : (p + 1) * 128]
            if p == 0:
                bufS[dp, cy, cx, cc, :, i * 128 : (i + 1) * 128] = block
            else:
                bufW[p - 1, dp, cy, cx, cc, :, i * 128 : (i + 1) * 128] = block
    bufS[dp, cy, cx, cc, :, 384:512] = gains[...]

    barrier = pltpu.get_barrier_semaphore()
    greet = [place.along(k + 1) for k in range(dpn - 1)]
    greet += [place.across(Y), place.across(X), place.across(C), nxt, prv]
    for device in greet:
        pl.semaphore_signal(barrier, inc=1, device_id=device, device_id_type=MESH)
    pl.semaphore_wait(barrier, len(greet))

    bufs = {W0: bufS, O: bufO}
    for k in range(3):
        bufs[W1 + k] = bufW.at[k]
    for k in range(2):
        bufs[T0 + k] = bufT.at[k]
        bufs[U0 + k] = bufU.at[k]
    for k in range(4):
        bufs[I0 + k] = bufI.at[k]
    comm = {}
    for k, (name, order) in enumerate(GATHERS):
        comm[name] = Gather(place, bufs[name], ags.at[k], agr.at[k], order)
    for b in range(NB):
        comm[H0 + b] = Shift(remote(tok.at[b], tokP.at[b], hs.at[b], hr.at[b], nxt))
        comm[B0 + b] = Shift(remote(tokP.at[b], hgR.at[b], hs.at[2 + b], hr.at[2 + b], prv))
    kept = []

    def sink(name):
        def put(total):
            if name < RU0:
                k = name - RI0
                gi[:, k * 512 : (k + 1) * 512] = total
            elif name < RO:
                k = name - RU0
                gu[:, k * 256 : (k + 1) * 256] = total
            elif name == RO:
                go_[...] = total[:, 0:512]
                kept.append(total[:, 513:514])
            else:
                at = slice((name - RQ0) * 128, (name - RQ0 + 1) * 128)
                for i, grad in enumerate((gq, gk, gv)):
                    grad[:, at] = total[:, i * 128 : (i + 1) * 128]

        return put

    accs = {RO: bufO}
    for k in range(2):
        accs[RU0 + k] = bufU.at[k]
    for k in range(4):
        accs[RI0 + k] = bufI.at[k]
        accs[RQ0 + k] = near.at[0, k, :, :, :, :, :, 0:384]
    for k, (name, order) in enumerate(SUMS):
        comm[name] = Scatter(place, accs[name], recvs[k], rss.at[k], rsr.at[k], order, sink(name))

    def tick(*label):
        for name in PLAN.get(label, ()):
            comm[name].advance()

    def need(label, *names):
        for name in BEFORE.get(label, ()):
            comm[name].advance()
        for name in names:
            comm[name].finish()

    bufO[dp, cy, cx, cc, :, 0:512] = wo[...]
    bufO[dp, cy, cx, cc, :, 512:640] = gains[...]
    for j in range(4):
        bufI[j, dp, cy, cx, cc] = wi[:, j * 512 : (j + 1) * 512]
    for q in range(2):
        bufU[q, dp, cy, cx, cc] = wu[:, q * 256 : (q + 1) * 256]
    for q in range(2):
        bufT[q, cy, cx, cc] = tab[:, q * 256 : (q + 1) * 256]
    tick(BEGIN)

    seg = s
    base = seg * SEG
    away = (seg == 0).astype(f32) * far

    def set_bias(b):
        q = lax.broadcasted_iota(jnp.int32, (1, SEG), 1)
        k = lax.broadcasted_iota(jnp.int32, (SEG, SEG), 0)
        limit = jnp.where(base + q < pre[b], jnp.maximum(q, pre[b] - 1 - base), q)
        bias[b] = jnp.where(k <= limit, 0.0, -far).astype(f32)

    cot_in = []
    for b in range(NB):
        tok_in[b].wait()
        xT[b] = stage[b].T
        cot_in.append(pltpu.make_async_copy(cot.at[b], stage.at[b], dms.at[b]))
        cot_in[b].start()
        tick(XT, b)
    set_bias(0)
    tick(BIAS, 0)
    for b in range(NB):
        cot_in[b].wait()
        coT[b] = stage[b].T
        tick(COT, b)
    set_bias(1)
    tick(BIAS, 1)
    need((NORM, 0), W0)

    again = bufS[..., 384:512].reshape(D, 128)[:, 0:1].astype(f32)

    def w3(p):
        return (bufS[..., 0:384] if p == 0 else bufW[p - 1]).reshape(D, 384)

    def own_norm(b):
        X = xT[b].astype(f32)
        niO[b] = (X * norm_scale(X) * again).astype(bf16)

    def own_proj(b, p):
        w = w3(p)
        kvO[b, p] = mm(niO[b], w[:, 128:384], 0, 0).astype(bf16)
        qs[b, p] = mm(w[:, 0:128], niO[b], 0, 0).astype(bf16) * jnp.asarray(0.125, bf16)

    def prev_norm(b):
        X = tokP[b].T.astype(f32)
        niP[b] = (X * norm_scale(X) * again).astype(bf16)

    def prev_proj(b, p):
        kvP[b, p] = mm(niP[b], w3(p)[:, 128:384], 0, 0).astype(bf16)

    def attend_own(b, p):
        ko, vo = kvO[b, p, :, 0:128], kvO[b, p, :, 128:256].T
        q2 = qs[b, p]
        for e in range(2):
            so = mm(ko, one_head(q2, e), 1, 0) + bias[b]
            top = jnp.max(so, axis=0, keepdims=True)
            eo = jnp.exp(so - top)
            rows = slice(e * HD, (e + 1) * HD)
            lse[b, 2 * p + e : 2 * p + e + 1, :] = top
            dlt[b, 2 * p + e : 2 * p + e + 1, :] = jnp.sum(eo, axis=0, keepdims=True)
            loc[b, p, rows] = mm(vo[rows], eo.astype(bf16), 1, 0)

    def attend_prev(b, p):
        kp, vp = kvP[b, p, :, 0:128], kvP[b, p, :, 128:256].T
        q2 = qs[b, p]
        for e in range(2):
            sp = mm(kp, one_head(q2, e), 1, 0)
            first = lse[b, 2 * p + e : 2 * p + e + 1, :]
            top = jnp.maximum(first, jnp.max(sp, axis=0, keepdims=True) - away)
            ep = jnp.exp(sp - (top + away))
            keep = jnp.exp(first - top)
            total = dlt[b, 2 * p + e : 2 * p + e + 1, :] * keep + jnp.sum(ep, axis=0, keepdims=True)
            rows = slice(e * HD, (e + 1) * HD)
            o = loc[b, p, rows] * keep + mm(vp[rows], ep.astype(bf16), 1, 0)
            loc[b, p, rows] = o / total
            lse[b, 2 * p + e : 2 * p + e + 1, :] = top + jnp.log(total)

    def remember(b):
        halves = [bufT[h].reshape(-1, 256) for h in range(2)]
        q = qs[b].reshape(D, SEG).astype(f32)
        row = lax.broadcasted_iota(jnp.int32, (halves[0].shape[0], SEG), 0)
        scores = []
        for k in range(KNN):
            hot = (row == nbr[b, k : k + 1, :]).astype(bf16)
            rows = jnp.concatenate([mm(half, hot, 0, 0) for half in halves], axis=0)
            near[b, k] = rows.astype(bf16).reshape(lead + (16, SEG))
            scores.append(per_head(q * rows))
        top = scores[0]
        for k in range(1, KNN):
            top = jnp.maximum(top, scores[k])
        scores = [jnp.exp(v - top) for v in scores]
        total = scores[0] + scores[1] + scores[2] + scores[3]
        for k in range(KNN):
            nw[b, k] = scores[k] / total

    def blend(b):
        cols = bufS[..., 384:512].reshape(D, 128).astype(f32)
        gvec, fgain = cols[:, 1:2], cols[:, 2:3]
        recalled = spread(nw[b, 0]) * near[b, 0].reshape(D, SEG).astype(f32)
        for k in range(1, KNN):
            recalled = recalled + spread(nw[b, k]) * near[b, k].reshape(D, SEG).astype(f32)
        local = loc[b].reshape(D, SEG)
        opened = jax.nn.sigmoid(per_head(local * gvec))
        gate[b] = opened
        wide = spread(opened)
        blended = (wide * recalled + (1.0 - wide) * local).astype(bf16)
        bld[b] = blended
        w = bufO[..., 0:512].reshape(D, D)
        middle = xT[b].astype(f32) + mm(w, blended, 0, 0)
        mid[b] = middle
        y[b] = middle
        fi[b] = (middle * norm_scale(middle) * fgain).astype(bf16)

    for b in range(NB):
        own_norm(b)
        tick(NORM, b)
    for p in range(PAIRS):
        for b in range(NB):
            need((PROJ, b, p), W0 + p)
            own_proj(b, p)
            tick(PROJ, b, p)
        for b in range(NB):
            attend_own(b, p)
            tick(OWN, b, p)

    def previous(b):
        need((PN, b), H0 + b)
        prev_norm(b)
        tick(PN, b)
        for p in range(PAIRS):
            prev_proj(b, p)
        tick(PP, b)
        for p in range(PAIRS):
            attend_prev(b, p)
            tick(PREV, b, p)

    for kind, b in FORWARD:
        if kind == PREV:
            previous(b)
        elif kind == REM:
            need((REM, b), T0, T1)
            remember(b)
            tick(REM, b)
        else:
            need((BLEND, b), O)
            blend(b)
            tick(BLEND, b)

    root = 0.7978845608028654
    def ffn(j, b):
        win = bufI[j].reshape(D, 512)
        wout = [bufU[q, j].reshape(512, 256) for q in range(2)]
        v = mm(win, fi[b], 0, 0)
        gh = mm(wout[0], coT[b, 0:256], 1, 0) + mm(wout[1], coT[b, 256:512], 1, 0)
        v2 = v * v
        t = jnp.tanh(root * v * (1.0 + 0.044715 * v2))
        half = 0.5 * (1.0 + t)
        hb = (v * half).astype(bf16)
        G[b, j, 0:512] = hb
        slope = half + 0.5 * v * (1.0 - t * t) * (root * (1.0 + 3 * 0.044715 * v2))
        gp = (gh * slope).astype(bf16)
        for q in range(2):
            at = slice(q * 256, (q + 1) * 256)
            y[b, at] = y[b, at] + mm(wout[q], hb, 0, 0)
        into = mm(win, gp, 1, 0)
        if j == 0:
            gm[b] = into
        else:
            gm[b] = gm[b] + into
        return gp

    for j in range(4):
        gps = []
        for b in range(NB):
            need((FFN, j, b), U0, U1, I0 + j)
            gps.append(ffn(j, b))
            tick(FFN, j, b)
        gin = mm(fi[0], gps[0], 1, 1) + mm(fi[1], gps[1], 1, 1)
        comm[I0 + j].drain()
        bufI[j] = gin.astype(bf16).reshape(lead + (16, 512))
        tick(GIN, j)
    for name, order in GATHERS:
        if not I0 <= name <= I3:
            comm[name].drain()
    for b in range(NB):
        comm[H0 + b].drain()
    for q in range(2):
        at = slice(q * 256, (q + 1) * 256)
        a = mm(G[0, :, 0:512].reshape(FF, SEG), coT[0, at], 1, 1)
        a = a + mm(G[1, :, 0:512].reshape(FF, SEG), coT[1, at], 1, 1)
        bufU[q] = a.astype(bf16).reshape(lead + (64, 256))
        tick(UG, q)

    out_copies = []
    cols = bufS[..., 384:512].reshape(D, 128).astype(f32)
    gvec, fgain = cols[:, 1:2], cols[:, 2:3]
    wout_a = bufO[..., 0:512].reshape(D, D)
    gwo = None
    ggv = None
    for b in range(NB):
        stage[b] = y[b].astype(bf16).T
        copy = pltpu.make_async_copy(stage.at[b], out.at[b], dms.at[b])
        copy.start()
        out_copies.append(copy)
        middle = mid[b]
        scale = norm_scale(middle)
        grad = coT[b].astype(f32) + norm_back(gm[b] * fgain, middle * scale, scale)
        gm[b] = grad
        gb = grad.astype(bf16)
        part = mm(bld[b], gb, 1, 1)
        gwo = part if gwo is None else gwo + part
        gbl = mm(wout_a, gb, 1, 0)
        local = loc[b].reshape(D, SEG)
        opened = gate[b]
        along = per_head(gbl * local)
        hits = [per_head(gbl * near[b, k].reshape(D, SEG).astype(f32)) for k in range(KNN)]
        mixed = hits[0] * nw[b, 0]
        for k in range(1, KNN):
            mixed = mixed + hits[k] * nw[b, k]
        ggate = (mixed - along) * opened * (1.0 - opened)
        wide = spread(ggate)
        part = jnp.sum(wide * local, axis=1, keepdims=True)
        ggv = part if ggv is None else ggv + part
        dlo = (spread(1.0 - opened) * gbl + wide * gvec).astype(bf16)
        fi[b] = dlo
        dots = per_head(dlo.astype(f32) * local)
        dlt[b] = dots
        dq = None
        for k in range(KNN):
            weight = spread(nw[b, k] * opened * (hits[k] - mixed) * 0.125)
            part = weight * near[b, k].reshape(D, SEG).astype(f32)
            dq = part if dq is None else dq + part
        y[b] = dq
        tick(CPRE, b)
    bufO[..., 0:512] = gwo.astype(bf16).reshape(lead + (16, 512))
    bufO[..., 512:640] = jnp.broadcast_to(ggv, (D, 128)).astype(bf16).reshape(lead + (16, 128))
    tick(GWO)

    def retreat(b, p, kv, own):
        k2, v2 = kv[b, p, :, 0:128], kv[b, p, :, 128:256]
        kt = k2.T
        q2 = qs[b, p]
        d2 = fi[b, pl.ds(p * 128, 128), :]
        for e in range(2):
            rows = slice(e * HD, (e + 1) * HD)
            sc = mm(k2, one_head(q2, e), 1, 0)
            if own:
                pr = jnp.exp((sc + bias[b]) - lse[b, 2 * p + e : 2 * p + e + 1, :])
            else:
                pr = jnp.exp(sc - (lse[b, 2 * p + e : 2 * p + e + 1, :] + away))
            dpr = mm(v2, one_head(d2, e), 1, 0)
            ds = (pr * (dpr - dlt[b, 2 * p + e : 2 * p + e + 1, :])).astype(bf16)
            dv = mm(d2[rows], pr.astype(bf16), 1, 1).astype(bf16)
            dk = mm(q2[rows], ds, 1, 1).astype(bf16)
            dq = mm(kt[rows], ds, 1, 0) * 0.125
            at = pl.ds(p * 128 + e * HD, HD)
            low, high = e * HD, (e + 1) * HD
            if own:
                G[b, p, low:high] = (y[b, at, :] + dq).astype(bf16)
                G[b, p, 128 + low : 128 + high] = dk
                G[b, p, 256 + low : 256 + high] = dv
            else:
                y[b, at, :] = y[b, at, :] + dq
                G[b, p, 384 + low : 384 + high] = dk
                G[b, p, 512 + low : 512 + high] = dv

    def send_back(b):
        sent = mm(w3(0)[:, 128:384], G[b, 0, 384:640], 1, 0)
        for p in range(1, PAIRS):
            sent = sent + mm(w3(p)[:, 128:384], G[b, p, 384:640], 1, 0)
        tokP[b] = sent.astype(bf16)

    for b in range(NB):
        for p in range(PAIRS):
            retreat(b, p, kvP, False)
            tick(RP, b, p)
        send_back(b)
        tick(SEND, b)
    for p in range(PAIRS):
        for b in range(NB):
            retreat(b, p, kvO, True)
            tick(ROW, b, p)
        quer = mm(niO[0], G[0, p, 0:128], 1, 1) + mm(niO[1], G[1, p, 0:128], 1, 1)
        near[0, p, ..., 0:128] = quer.astype(bf16).reshape(lead + (16, 128))
        rest = mm(niO[0], G[0, p, 128:384], 1, 1)
        rest = rest + mm(niP[0], G[0, p, 384:640], 1, 1)
        rest = rest + mm(niO[1], G[1, p, 128:384], 1, 1)
        rest = rest + mm(niP[1], G[1, p, 384:640], 1, 1)
        near[0, p, ..., 128:384] = rest.astype(bf16).reshape(lead + (16, 256))
        tick(DW, p)

    def finish(b):
        total = mm(w3(0), G[b, 0, 0:384], 1, 0)
        for p in range(1, PAIRS):
            total = total + mm(w3(p), G[b, p, 0:384], 1, 0)
        total = total + hgR[b].astype(f32)
        X = xT[b].astype(f32)
        scale = norm_scale(X)
        res = gm[b] + norm_back(total * again, X * scale, scale)
        mid[b] = res.T
        copy = pltpu.make_async_copy(mid.at[b], ig.at[b], dms.at[2 + b])
        copy.start()
        return copy

    ends = []
    for b in range(NB):
        need((FIN, b), B0 + b)
        ends.append(finish(b))
        tick(FIN, b)
    need((END,), *(name for name, order in SUMS))
    own = gains[...].astype(f32)
    fsum = jnp.sum(gi[...] * wi[...].astype(f32), axis=1, keepdims=True) / own[:, 2:3]
    asum = gq[...] * wq[...].astype(f32) + gk[...] * wk[...].astype(f32) + gv[...] * wv[...].astype(f32)
    asum = jnp.sum(asum, axis=1, keepdims=True) / own[:, 0:1]
    lane = lax.broadcasted_iota(jnp.int32, (16, 128), 1)
    here = lax.broadcasted_iota(jnp.int32, (16, 128), 0) == lane
    for i, col in enumerate((asum, kept[0], fsum)):
        gg[i : i + 1, :] = jnp.sum(jnp.where(here, col, 0.0), axis=0, keepdims=True)
    for name, order in SUMS:
        comm[name].drain()
    for b in range(NB):
        comm[B0 + b].drain()
    for copy in out_copies + ends:
        copy.wait()


def fused(dpn, tokens, prefix, neighbours, table, attn_gain, w_query, w_key, w_value, gate_vector,
          w_output, ffn_gain, w_inner, w_outer, cotangent):
    gains = jnp.pad(jnp.stack([attn_gain, gate_vector, ffn_gain], axis=1), ((0, 0), (0, 125)))
    vm = pl.BlockSpec(memory_space=pltpu.VMEM)
    hb = pl.BlockSpec(memory_space=pl.ANY)
    sm = pl.BlockSpec(memory_space=pltpu.SMEM)
    V = pltpu.VMEM
    lead = (dpn, 2, 2, 2)
    sq = (NB, D, SEG)

    sizes = {Z: dpn, Y: 2, X: 2, C: 2}

    def landing(name, order):
        if name < RU0:
            block = (16, 512)
        elif name < RO:
            block = (64, 256)
        else:
            block = (16, 640) if name == RO else (16, 384)
        shapes = []
        for stage, axis in enumerate(order):
            left = tuple(sizes[a] for a in AXES if a not in order[: stage + 1])
            shapes.append(V((sizes[axis] - 1,) + left + block, bf16))
        return shapes

    scratch = [
        V(lead + (16, 512), bf16),
        V((PAIRS - 1,) + lead + (16, 384), bf16),
        V(lead + (16, 640), bf16),
        V((4,) + lead + (16, 512), bf16),
        V((2,) + lead + (64, 256), bf16),
        V((2, 2, 2, 2, table.shape[0], 256), bf16),
        V(sq, bf16),
        V(sq, bf16),
        V(sq, bf16),
        V(sq, bf16),
        V(sq, bf16),
        V(sq, bf16),
        V((NB, PAIRS, 128, SEG), bf16),
        V((NB, PAIRS, SEG, 256), bf16),
        V((NB, PAIRS, SEG, 256), bf16),
        V((NB, PAIRS, 128, SEG), f32),
        V((NB, KNN) + lead + (16, SEG), bf16),
        V((NB, KNN, HEADS, SEG), f32),
        V((NB, HEADS, SEG), f32),
        V((NB, HEADS, SEG), f32),
        V((NB, HEADS, SEG), f32),
        V(sq, f32),
        V(sq, bf16),
        V(sq, bf16),
        V(sq, f32),
        V(sq, f32),
        V((NB, SEG, SEG), f32),
        V((NB, PAIRS, 640, SEG), bf16),
        V(sq, bf16),
    ]
    for name, order in SUMS:
        scratch += landing(name, order)
    dma = pltpu.SemaphoreType.DMA
    scratch += [
        dma((len(GATHERS), dpn + 2)), dma((len(GATHERS), dpn + 2)), dma((len(SUMS), dpn + 2)),
        dma((len(SUMS), dpn + 2)), dma((4,)), dma((4,)), dma((4,)),
    ]
    rows = w_query.shape[0]
    sds = jax.ShapeDtypeStruct
    out = pl.pallas_call(
        lambda *refs: layer(dpn, *refs),
        name="layer",
        out_shape=(
            sds(tokens.shape, bf16),
            sds(tokens.shape, f32),
            sds((rows, D), f32),
            sds((rows, D), f32),
            sds((rows, D), f32),
            sds((rows, D), f32),
            sds((rows, FF), f32),
            sds(w_outer.shape, f32),
            sds((8, 128), f32),
        ),
        in_specs=[hb, sm, vm, vm, vm, vm, vm, vm, vm, vm, vm, hb],
        out_specs=(hb, hb) + (vm,) * 7,
        scratch_shapes=scratch,
        compiler_params=pltpu.CompilerParams(
            collective_id=0, has_side_effects=True, vmem_limit_bytes=63 * 2**20
        ),
    )(
        tokens, prefix, neighbours.transpose(0, 2, 1), table, gains, w_query, w_key, w_value, w_output,
        w_inner, w_outer, cotangent,
    )
    return settle(out)


def settle_kernel(*refs):
    big, gg = refs[:8], refs[8]
    to, vectors = refs[9:17], refs[17:20]
    bufs, sems, outs = refs[20:28], refs[28], refs[29]
    pieces = []
    for src, buf, dst in zip(big, bufs, to):
        if len(src.shape) == 3:
            for i in range(2):
                for j in range(2):
                    at = (i, pl.ds(j * 256, 256))
                    pieces.append((src.at[at], buf.at[at], dst.at[at]))
        else:
            pieces.append((src, buf, dst))
    come = [pltpu.make_async_copy(a, b, sems.at[k]) for k, (a, b, c) in enumerate(pieces)]
    leave = [pltpu.make_async_copy(b, c, outs.at[k]) for k, (a, b, c) in enumerate(pieces)]
    for copy in come:
        copy.start()
    for i, vector in enumerate(vectors):
        vector[...] = gg[i, 0:16]
    for first, then in zip(come, leave):
        first.wait()
        then.start()
    for copy in leave:
        copy.wait()


def settle(out):
    hb = pl.BlockSpec(memory_space=pl.ANY)
    vm = pl.BlockSpec(memory_space=pltpu.VMEM)
    sds = jax.ShapeDtypeStruct
    res = pl.pallas_call(
        settle_kernel,
        name="settle",
        out_shape=tuple(sds(v.shape, v.dtype) for v in out[:8]) + (sds((16,), f32),) * 3,
        in_specs=[hb] * 8 + [vm],
        out_specs=(hb,) * 8 + (vm,) * 3,
        scratch_shapes=[pltpu.VMEM(v.shape, v.dtype) for v in out[:8]]
        + [pltpu.SemaphoreType.DMA((14,)), pltpu.SemaphoreType.DMA((14,))],
    )(*out)
    return (
        res[0], res[1], res[8], res[2], res[3], res[4], res[9], res[5], res[10], res[6], res[7],
    )


masked_floor = -1000000000.0


def from_behind(value, axis, by):
    count = lax.axis_size(axis)
    pairs = [(i, i + by) for i in range(count) if 0 <= i + by < count]
    return lax.ppermute(value, axis, pairs)


def times_plain(left, right):
    return jnp.dot(left, right, preferred_element_type=jnp.float32)


def times_first_t(left, right):
    return lax.dot_general(
        left, right, (((0,), (0,)), ((), ())), preferred_element_type=jnp.float32
    )


def times_second_t(left, right):
    return lax.dot_general(
        left, right, (((1,), (1,)), ((), ())), preferred_element_type=jnp.float32
    )


def gelu_tanh(values):
    return jax.nn.gelu(values, approximate=True)


def rms_scale(values):
    return lax.rsqrt(jnp.mean(values * values, axis=-1, keepdims=True) + epsilon)


def norm_back_rows(grad_normed, normed, scale):
    return scale * (grad_normed - normed * jnp.mean(grad_normed * normed, axis=-1, keepdims=True))


def split_heads(rows):
    return rows.reshape(rows.shape[0], HEADS, HD).transpose(1, 0, 2)


def merge_heads(stacked):
    return stacked.transpose(1, 0, 2).reshape(stacked.shape[1], D)


def visible_mask(segment, prefix_len):
    query_pos = segment * SEG + lax.iota(jnp.int32, SEG)
    key_pos = (segment - 1) * SEG + lax.iota(jnp.int32, 2 * SEG)
    return (key_pos[None, :] >= 0) & (
        (key_pos[None, :] <= query_pos[:, None])
        | (query_pos[:, None] < prefix_len) & (key_pos[None, :] < prefix_len)
    )


def fetch_attention(attn_gain, w_query, w_key, w_value, gate_vector, w_output):
    return (
        lax.all_gather(attn_gain, ("dp", "seq"), axis=0, tiled=True),
        lax.all_gather(w_query, ("dp", "seq"), axis=0, tiled=True),
        lax.all_gather(w_key, ("dp", "seq"), axis=0, tiled=True),
        lax.all_gather(w_value, ("dp", "seq"), axis=0, tiled=True),
        lax.all_gather(gate_vector, ("dp", "seq"), axis=0, tiled=True),
        lax.all_gather(w_output, ("dp", "seq"), axis=0, tiled=True),
    )


def fetch_feedforward(ffn_gain, w_inner, w_outer):
    return (
        lax.all_gather(ffn_gain, ("dp", "seq"), axis=0, tiled=True),
        lax.all_gather(w_inner, ("dp", "seq"), axis=0, tiled=True),
        lax.all_gather(w_outer, ("dp", "seq"), axis=0, tiled=True),
    )


def forward_pass(tokens_row, visible, near_b, attn_set, ffn_set):
    attn_gain, w_query, w_key, w_value, gate_vector, w_output = attn_set
    ffn_gain, w_inner, w_outer = ffn_set
    rows_count = tokens_row.shape[0]
    inputs_f = tokens_row.astype(jnp.float32)
    scale_one = rms_scale(inputs_f)
    normed_one = inputs_f * scale_one
    normed_in = (normed_one * attn_gain.astype(jnp.float32)).astype(jnp.bfloat16)
    query_b = times_plain(normed_in, w_query).astype(jnp.bfloat16)
    key_b = times_plain(normed_in, w_key).astype(jnp.bfloat16)
    value_b = times_plain(normed_in, w_value).astype(jnp.bfloat16)
    key_prev, value_prev = from_behind((key_b, value_b), "seq", 1)
    key_all = jnp.concatenate([key_prev, key_b], axis=0)
    value_all = jnp.concatenate([value_prev, value_b], axis=0)
    visible_f = visible.astype(jnp.float32)

    def head_forward(operands):
        query_h, key_h, value_h = operands
        scores = jnp.where(visible, times_second_t(query_h, key_h) * 0.125, masked_floor)
        row_max = jnp.max(scores, axis=1, keepdims=True)
        exponent = jnp.exp(scores - row_max) * visible_f
        row_sum = jnp.sum(exponent, axis=1, keepdims=True)
        attn_probs = (exponent / row_sum).astype(jnp.bfloat16)
        return (times_plain(attn_probs, value_h), (row_max + jnp.log(row_sum))[:, 0])

    local_h, log_norm = lax.map(
        head_forward, (split_heads(query_b), split_heads(key_all), split_heads(value_all))
    )
    local_t = local_h.transpose(1, 0, 2)
    query_t = query_b.reshape(rows_count, HEADS, HD)
    near_scores = (
        jnp.einsum("shd,skhd->shk", query_t, near_b, preferred_element_type=jnp.float32) * 0.125
    )
    near_exp = jnp.exp(near_scores - jnp.max(near_scores, axis=-1, keepdims=True))
    near_weights = near_exp / jnp.sum(near_exp, axis=-1, keepdims=True)
    recalled = jnp.einsum("shk,skhd->shd", near_weights, near_b, preferred_element_type=jnp.float32)
    gate_h = gate_vector.astype(jnp.float32).reshape(HEADS, HD)
    gate_open = jax.nn.sigmoid(jnp.sum(local_t * gate_h, axis=-1, keepdims=True))
    blended_b = (
        (gate_open * recalled + (1.0 - gate_open) * local_t)
        .reshape(rows_count, D)
        .astype(jnp.bfloat16)
    )
    middle = inputs_f + times_plain(blended_b, w_output)
    scale_two = rms_scale(middle)
    normed_two = middle * scale_two
    ffn_in = (normed_two * ffn_gain.astype(jnp.float32)).astype(jnp.bfloat16)
    hidden_pre = times_plain(ffn_in, w_inner)
    hidden_b = gelu_tanh(hidden_pre).astype(jnp.bfloat16)
    result = (middle + times_plain(hidden_b, w_outer)).astype(jnp.bfloat16)
    kept = (
        scale_one,
        normed_one,
        normed_in,
        query_b,
        key_all,
        value_all,
        log_norm,
        local_t,
        near_weights,
        recalled,
        gate_open,
        blended_b,
        scale_two,
        normed_two,
        ffn_in,
        hidden_pre,
        hidden_b,
    )
    return (result, kept)


def backward_pass(kept, cot_row, visible, near_b, attn_set, ffn_set):
    (
        scale_one,
        normed_one,
        normed_in,
        query_b,
        key_all,
        value_all,
        log_norm,
        local_t,
        near_weights,
        recalled,
        gate_open,
        blended_b,
        scale_two,
        normed_two,
        ffn_in,
        hidden_pre,
        hidden_b,
    ) = kept
    attn_gain, w_query, w_key, w_value, gate_vector, w_output = attn_set
    ffn_gain, w_inner, w_outer = ffn_set
    rows_count = cot_row.shape[0]
    dout = cot_row.astype(jnp.float32)
    grad_outer = times_first_t(hidden_b, cot_row)
    grad_hidden = times_second_t(cot_row, w_outer)
    unused_value, gelu_pull = jax.vjp(gelu_tanh, hidden_pre)
    grad_pre = gelu_pull(grad_hidden)[0].astype(jnp.bfloat16)
    grad_inner = times_first_t(ffn_in, grad_pre)
    grad_ffn_in = times_second_t(grad_pre, w_inner)
    grad_ffn_gain = jnp.sum(grad_ffn_in * normed_two, axis=0)
    grad_middle = dout + norm_back_rows(
        grad_ffn_in * ffn_gain.astype(jnp.float32), normed_two, scale_two
    )
    grad_branch_b = grad_middle.astype(jnp.bfloat16)
    grad_output = times_first_t(blended_b, grad_branch_b)
    grad_blended = times_second_t(grad_branch_b, w_output).reshape(rows_count, HEADS, HD)
    gate_h = gate_vector.astype(jnp.float32).reshape(HEADS, HD)
    grad_recalled = gate_open * grad_blended
    grad_gate = (
        jnp.sum(grad_blended * (recalled - local_t), axis=-1, keepdims=True)
        * gate_open
        * (1.0 - gate_open)
    )
    grad_gate_vector = jnp.sum(grad_gate * local_t, axis=0).reshape(D)
    grad_local_b = (
        ((1.0 - gate_open) * grad_blended + grad_gate * gate_h)
        .astype(jnp.bfloat16)
        .transpose(1, 0, 2)
    )
    grad_near_w = jnp.einsum(
        "shd,skhd->shk", grad_recalled, near_b, preferred_element_type=jnp.float32
    )
    grad_near = near_weights * (
        grad_near_w - jnp.sum(near_weights * grad_near_w, axis=-1, keepdims=True)
    )
    grad_query_near = (
        jnp.einsum("shk,skhd->shd", grad_near, near_b, preferred_element_type=jnp.float32) * 0.125
    )
    visible_f = visible.astype(jnp.float32)

    def head_backward(operands):
        query_h, key_h, value_h, grad_h, norm_h = operands
        scores = jnp.where(visible, times_second_t(query_h, key_h) * 0.125, masked_floor)
        attn_probs = jnp.exp(scores - norm_h[:, None]) * visible_f
        grad_probs = times_second_t(grad_h, value_h)
        grad_scores = (
            attn_probs * (grad_probs - jnp.sum(attn_probs * grad_probs, axis=1, keepdims=True))
        ).astype(jnp.bfloat16)
        return (
            times_plain(grad_scores, key_h) * 0.125,
            times_first_t(grad_scores, query_h) * 0.125,
            times_first_t(attn_probs.astype(jnp.bfloat16), grad_h),
        )

    grad_query_h, grad_key_h, grad_value_h = lax.map(
        head_backward,
        (
            split_heads(query_b),
            split_heads(key_all),
            split_heads(value_all),
            grad_local_b,
            log_norm,
        ),
    )
    grad_key_all = merge_heads(grad_key_h)
    grad_value_all = merge_heads(grad_value_h)
    later_key, later_value = (
        from_behind(grad_key_all[:rows_count].astype(jnp.bfloat16), "seq", -1).astype(jnp.float32),
        from_behind(grad_value_all[:rows_count].astype(jnp.bfloat16), "seq", -1).astype(
            jnp.float32
        ),
    )
    grad_query_b = (merge_heads(grad_query_h) + grad_query_near.reshape(rows_count, D)).astype(
        jnp.bfloat16
    )
    grad_key_b = (grad_key_all[rows_count:] + later_key).astype(jnp.bfloat16)
    grad_value_b = (grad_value_all[rows_count:] + later_value).astype(jnp.bfloat16)
    grad_query = times_first_t(normed_in, grad_query_b)
    grad_key = times_first_t(normed_in, grad_key_b)
    grad_value = times_first_t(normed_in, grad_value_b)
    grad_normed_in = (
        times_second_t(grad_query_b, w_query)
        + times_second_t(grad_key_b, w_key)
        + times_second_t(grad_value_b, w_value)
    )
    grad_attn_gain = jnp.sum(grad_normed_in * normed_one, axis=0)
    input_grad = grad_middle + norm_back_rows(
        grad_normed_in * attn_gain.astype(jnp.float32), normed_one, scale_one
    )
    grads = (
        grad_attn_gain,
        grad_query,
        grad_key,
        grad_value,
        grad_gate_vector,
        grad_output,
        grad_ffn_gain,
        grad_inner,
        grad_outer,
    )
    return (grads, input_grad)


def plain(
    tokens,
    prefix,
    neighbours,
    table,
    attn_gain,
    w_query,
    w_key,
    w_value,
    gate_vector,
    w_output,
    ffn_gain,
    w_inner,
    w_outer,
    cotangent,
):
    full_table = lax.all_gather(table, "seq", axis=0, tiled=True)
    segment = lax.axis_index("seq")
    rows_count = tokens.shape[1]
    outputs = []
    input_grads = []
    running = ()
    for micro_batch in range(tokens.shape[0]):
        visible = visible_mask(segment, prefix[micro_batch])
        near_b = jnp.take(full_table, neighbours[micro_batch].reshape(-1), axis=0).reshape(
            rows_count, KNN, HEADS, HD
        )
        attn_fwd = fetch_attention(attn_gain, w_query, w_key, w_value, gate_vector, w_output)
        ffn_fwd = fetch_feedforward(ffn_gain, w_inner, w_outer)
        result, kept = forward_pass(tokens[micro_batch], visible, near_b, attn_fwd, ffn_fwd)
        attn_back = fetch_attention(attn_gain, w_query, w_key, w_value, gate_vector, w_output)
        ffn_back = fetch_feedforward(ffn_gain, w_inner, w_outer)
        grads, input_grad = backward_pass(
            kept, cotangent[micro_batch], visible, near_b, attn_back, ffn_back
        )
        if micro_batch == 0:
            running = grads
        else:
            running = tuple((earlier + increment for earlier, increment in zip(running, grads)))
        outputs.append(result)
        input_grads.append(input_grad)
    shares = lax.psum_scatter(running, ("dp", "seq"), scatter_dimension=0, tiled=True)
    return (
        jnp.stack(outputs),
        jnp.stack(input_grads),
        shares[0],
        shares[1],
        shares[2],
        shares[3],
        shares[4],
        shares[5],
        shares[6],
        shares[7],
        shares[8],
    )


def solution(mesh):
    dpn = mesh.shape["dp"]

    def local(*args):
        if mesh.shape["seq"] == 8 and args[5].shape[0] == 16:
            return fused(dpn, *args)
        return plain(*args)

    rows = P(("dp", "seq"))
    wide = P(("dp", "seq"), None)
    block = P("dp", "seq", None)
    return jax.shard_map(
        local,
        mesh=mesh,
        in_specs=(
            block, P("dp"), block, P("seq", None), rows, wide, wide, wide, rows, wide, rows, wide, wide, block,
        ),
        out_specs=(block, block, rows, wide, wide, wide, rows, wide, rows, wide, wide),
        check_vma=False,
    )
```
